256 devices in a mesh: section: 8 (over z_lo, core), mesh: 32 (over x, z_hi, y).
Axes of the slice: x: 4, y: 4, z: 8 (z_hi: 2, z_lo: 4; z = z_hi * 4 + z_lo), core: 2. Of those that a mesh axis runs over, the one named last changes fastest.
Arguments:
- saved_inputs: bfloat16 [8, 3, 8192, 1024], P('section', None, 'mesh'), may hold values from -8 to 8
- w_query: bfloat16 [8, 1024, 1024], P('section'), may hold values from -6 to 6
- w_key: bfloat16 [8, 1024, 1024], P('section'), may hold values from -6 to 6
- w_value: bfloat16 [8, 1024, 1024], P('section'), may hold values from -0.1875 to 0.1875
- w_out: bfloat16 [8, 1024, 1024], P('section'), may hold values from -0.1875 to 0.1875
- pending: bfloat16 [8, 8192, 1024], P('section', 'mesh'), may hold values from -6 to 6
- top_grads: bfloat16 [1, 8192, 1024], P(None, 'mesh'), may hold values from -6 to 6
- key_blocks: int32 [64, 2], P('mesh'), may hold values from -1 to 63, as said below
- counts: int32 [64], replicated, may hold values from 64 to 128, as said below
- plan: int32 [2, 8], replicated, may hold values from 0 to 2
Outputs:
- layer_grads: float32 [8, 1024, 4, 1024], P('section', 'mesh')
- input_grads: bfloat16 [2, 8, 8192, 1024], P(None, 'section', 'mesh')
The draws below stay inside these ranges and needn't reach their ends.
Inputs may be any that keep to these rules, and one draw needn't show every extreme that they name: `key_blocks`: entry j of block b is -1 (nothing read) or the block (b + o_j) modulo 64, with o = (1, -1). `counts`: the padding nodes of a block are its last ones.
All inputs are finite; a program needn't handle non-finite values.
Results may differ from the reference program's by a relative error of at most 0.03.
The reference program's roundings to bfloat16 on the way count: a program that leaves them out, or rounds other values in their place, can miss the bound.
Values may be sent and summed in bfloat16 or wider, within the bound.
No kernel may reach another device: no remote copies, remote signals or barrier semaphores. Data moves between devices by JAX's collectives and lax.ppermute only.
A program may use at most 128 MiB of HBM per device.

```python
import math
import jax
import jax.numpy as jnp
import numpy as np
from jax import lax

D = 1024
HEADS = 8
HEAD_DIM = 128
BLOCK = 128
BLOCKS_DEV = 2
MEMBERS = 3
TICKS = 2
SECTIONS = 8
NODES = 8192


OFFSET_TABLE = (1, -1)


def draw_saved_inputs(key, part):
    full_shape = (SECTIONS, MEMBERS, NODES, D)
    normal_draw = jax.random.normal(jax.random.fold_in(key, 1), full_shape, jnp.float32)
    return jnp.clip(normal_draw, -6.0, 6.0).astype(jnp.bfloat16)


def projection_draw(key, salt):
    base = jax.random.normal(jax.random.fold_in(key, salt), (SECTIONS, D, D), jnp.float32) / math.sqrt(D)
    base = jnp.clip(base, -6.0 / math.sqrt(D), 6.0 / math.sqrt(D))
    return base


def draw_w_query(key, part):
    return projection_draw(key, 11).astype(jnp.bfloat16)


def draw_w_key(key, part):
    return projection_draw(key, 23).astype(jnp.bfloat16)


def draw_key_blocks(key, part):
    block_count = NODES // BLOCK
    offsets = jnp.array(OFFSET_TABLE, jnp.int32)
    owners = (jnp.arange(block_count, dtype=jnp.int32)[:, None] + offsets[None, :]) % block_count
    dice_rolls = jax.random.randint(jax.random.fold_in(key, 5), (block_count, 2), 0, 5)
    row_index = jnp.arange(block_count)[:, None]
    col_index = jnp.arange(2)[None, :]
    is_live = (dice_rolls < 3) | (row_index == 0)
    is_live = is_live & jnp.logical_not((row_index == 1) & (col_index == 0))
    return jnp.where(is_live, owners, -1).astype(jnp.int32)


def draw_counts(key, part):
    block_count = NODES // BLOCK
    drawn = jax.random.randint(jax.random.fold_in(key, 7), (block_count,), BLOCK // 2, BLOCK + 1)
    index_list = jnp.arange(block_count)
    drawn = jnp.where(index_list == 0, BLOCK, drawn)
    drawn = jnp.where(index_list == 1, BLOCK // 2, drawn)
    return drawn.astype(jnp.int32)


def place_ends(result, key, smallest, largest):
    longest = result.shape.index(max(result.shape))
    spots = []
    for shift in (0, 1):
        where = [jax.random.randint(jax.random.fold_in(key, axis), (), 0, length) for axis, length in enumerate(result.shape)]
        where[longest] = (where[longest] + shift) % result.shape[longest]
        spots.append(tuple(where))
    return result.at[spots[0]].set(smallest).at[spots[1]].set(largest)


def level_of(key, extent, cuts, low, top_value):
    def one(dim, shards_of):
        draws = jax.random.uniform(jax.random.fold_in(jax.random.fold_in(key, 6), dim), (shards_of,), jnp.float32, low / len(cuts), top_value / len(cuts))
        return jnp.repeat(jnp.exp(draws), extent[dim] // shards_of).reshape((-1,) + (1,) * (len(extent) - dim - 1))

    gain = one(*cuts[0])
    for cut in cuts[1:]:
        gain = gain * one(*cut)
    return gain


def gaussian(own_key, shape, deviation, bound, split=(), kind=jnp.bfloat16):
    values = jax.random.normal(own_key, shape, jnp.float32) * deviation
    if len(split) > 0:
        values = level_of(own_key, shape, split, -0.22, 0.18) * values
    return jnp.clip(values, min=-bound, max=bound).astype(kind)


def setup_inputs(seed: int = 0) -> dict:
    splits = jax.random.split(jax.random.key(seed), 11)
    return {
        "saved_inputs": draw_saved_inputs(jax.random.fold_in(splits[10], 71), 0),
        "w_query": draw_w_query(jax.random.fold_in(splits[10], 71), 0),
        "w_key": draw_w_key(jax.random.fold_in(splits[10], 71), 0),
        "w_value": gaussian(splits[3], (SECTIONS, D, D), D ** -0.5, 0.1875, ((0, 8),)),
        "w_out": gaussian(splits[4], (SECTIONS, D, D), D ** -0.5, 0.1875, ((0, 8),)),
        "pending": gaussian(splits[5], (SECTIONS, NODES, D), 1.0, 6.0, ((0, 8), (1, 32))),
        "top_grads": gaussian(splits[6], (TICKS - 1, NODES, D), 1.0, 6.0, ((1, 32),)),
        "key_blocks": draw_key_blocks(jax.random.fold_in(splits[10], 71), 0),
        "counts": draw_counts(jax.random.fold_in(splits[10], 71), 0),
        "plan": place_ends(jax.random.randint(splits[9], (TICKS, SECTIONS), 0, MEMBERS), jax.random.fold_in(splits[9], 1), 0, MEMBERS - 1).astype(jnp.int32),
    }


OFFSETS = (1, -1)
EPSILON = 1e-06

def right_dot(left, right):
    return lax.dot_general(left, right, (((1,), (1,)), ((), ())), preferred_element_type=jnp.float32)

def left_dot(left, right):
    return lax.dot_general(left, right, (((0,), (0,)), ((), ())), preferred_element_type=jnp.float32)

def round_trip(values):
    return lax.optimization_barrier(values.astype(jnp.bfloat16)).astype(jnp.float32)

def key_mask(key_blocks, counts):
    positions = jnp.arange(BLOCK)
    pieces = [positions[None, :] < counts[:, None]]
    for slot_index in range(len(OFFSETS)):
        listed = key_blocks[:, slot_index]
        remote_count = jnp.where(listed >= 0, counts[jnp.maximum(listed, 0)], 0)
        pieces.append(positions[None, :] < remote_count[:, None])
    return jnp.concatenate(pieces, axis=1)

def layer_back(x_in, query_weight, key_weight, value_weight, out_weight, upstream, mask):
    block_count = NODES // BLOCK
    part_count = block_count // BLOCKS_DEV
    slot_count = 1 + len(OFFSETS)
    score_scale = 1.0 / math.sqrt(HEAD_DIM)
    x_float = x_in.astype(jnp.float32)
    inv_rms = lax.rsqrt(lax.optimization_barrier(jnp.mean(x_float * x_float, axis=-1, keepdims=True)) + EPSILON)
    normed_float = x_float * inv_rms
    normed = normed_float.astype(jnp.bfloat16)
    queries = jnp.dot(normed, query_weight, preferred_element_type=jnp.float32).astype(jnp.bfloat16)
    key_rows = jnp.dot(normed, key_weight, preferred_element_type=jnp.float32).astype(jnp.bfloat16)
    value_rows = jnp.dot(normed, value_weight, preferred_element_type=jnp.float32).astype(jnp.bfloat16)

    def spread(rows):
        blocks = rows.reshape(block_count, BLOCK, D)
        listed = [blocks] + [jnp.roll(blocks, -offset, axis=0) for offset in OFFSETS]
        joined = jnp.concatenate(listed, axis=1)
        return joined.reshape(block_count, slot_count * BLOCK, HEADS, HEAD_DIM).astype(jnp.float32)
    keys_all = spread(key_rows)
    values_all = spread(value_rows)
    query_heads = queries.reshape(block_count, BLOCK, HEADS, HEAD_DIM).astype(jnp.float32)
    scores = jnp.einsum('pqhd,pkhd->phqk', query_heads, keys_all) * score_scale
    scores = jnp.where(mask[:, None, None, :], scores, -jnp.inf)
    peak = lax.optimization_barrier(jnp.max(scores, axis=-1, keepdims=True))
    raised = jnp.exp(scores - peak)
    probs = raised / lax.optimization_barrier(jnp.sum(raised, axis=-1, keepdims=True))
    probs_round = round_trip(probs)
    attended = jnp.einsum('phqk,pkhd->pqhd', probs_round, values_all).reshape(NODES, D).astype(jnp.bfloat16)
    grad_attended = right_dot(upstream, out_weight).astype(jnp.bfloat16)
    grad_heads = grad_attended.reshape(block_count, BLOCK, HEADS, HEAD_DIM).astype(jnp.float32)
    grad_probs = jnp.einsum('pqhd,pkhd->phqk', grad_heads, values_all)
    grad_scores = probs * (grad_probs - lax.optimization_barrier(jnp.sum(probs * grad_probs, axis=-1, keepdims=True))) * score_scale
    scores_round = round_trip(grad_scores)
    grad_query = jnp.einsum('phqk,pkhd->pqhd', scores_round, keys_all).reshape(NODES, D).astype(jnp.bfloat16)
    key_terms = jnp.einsum('phqk,pqhd->pkhd', scores_round, query_heads).reshape(block_count, slot_count, BLOCK, D)
    value_terms = jnp.einsum('phqk,pqhd->pkhd', probs_round, grad_heads).reshape(block_count, slot_count, BLOCK, D)
    block_owner = np.arange(block_count) // BLOCKS_DEV
    pair_terms = jnp.stack([key_terms, value_terms])
    local_sum = pair_terms[:, :, 0]
    from_before = jnp.zeros_like(local_sum)
    from_after = jnp.zeros_like(local_sum)
    for slot_index, offset in enumerate(OFFSETS):
        moved = jnp.roll(pair_terms[:, :, 1 + slot_index], offset, axis=1)
        source_owner = np.roll(block_owner, offset)
        delta = (source_owner - block_owner) % part_count
        same_mask = jnp.asarray(delta == 0)[None, :, None, None]
        before_mask = jnp.asarray(delta == part_count - 1)[None, :, None, None]
        after_mask = jnp.asarray(delta == 1)[None, :, None, None]
        local_sum = local_sum + jnp.where(same_mask, moved, 0.0)
        from_before = from_before + jnp.where(before_mask, moved, 0.0)
        from_after = from_after + jnp.where(after_mask, moved, 0.0)
    pair_total = local_sum + round_trip(from_before) + round_trip(from_after)
    grad_key = pair_total[0].reshape(NODES, D).astype(jnp.bfloat16)
    grad_value = pair_total[1].reshape(NODES, D).astype(jnp.bfloat16)
    grad_normed = right_dot(grad_query, query_weight) + right_dot(grad_key, key_weight) + right_dot(grad_value, value_weight)
    grad_input = inv_rms * (grad_normed - normed_float * lax.optimization_barrier(jnp.mean(grad_normed * normed_float, axis=-1, keepdims=True)))
    grad_x = (upstream.astype(jnp.float32) + grad_input).astype(jnp.bfloat16)
    return (grad_x, (normed, grad_query, grad_key, grad_value, attended, upstream))

def section_weights(stored):
    part_rows = BLOCKS_DEV * BLOCK
    part_count = NODES // part_rows

    def one_part(total, part_index):
        first_row = part_index * part_rows
        for terms in stored:
            rows = [lax.dynamic_slice_in_dim(array, first_row, part_rows, 0) for array in terms]
            normed, grad_query, grad_key, grad_value, attended, upstream = rows
            stacked = jnp.stack([left_dot(normed, grad_query), left_dot(normed, grad_key), left_dot(normed, grad_value), left_dot(attended, upstream)], axis=1)
            total = total + round_trip(stacked)
        return (total, None)
    return lax.scan(one_part, jnp.zeros((D, 4, D), jnp.float32), jnp.arange(part_count, dtype=jnp.int32))[0]

def reference(saved_inputs, w_query, w_key, w_value, w_out, pending, top_grads, key_blocks, counts, plan):
    mask = key_mask(key_blocks, counts)
    grads_by_section = [None] * SECTIONS
    inputs_by_section = [None] * SECTIONS
    from_above = None
    for section_index in range(SECTIONS - 1, -1, -1):
        outgoing = []
        stored = []
        for tick_index in range(TICKS):
            if tick_index == 0:
                upstream = pending[section_index]
            elif section_index == SECTIONS - 1:
                upstream = top_grads[tick_index - 1]
            else:
                upstream = from_above[tick_index - 1]
            member = plan[tick_index, section_index]
            x_in = lax.dynamic_index_in_dim(saved_inputs[section_index], member, 0, keepdims=False)
            grad_x, terms = layer_back(x_in, w_query[section_index], w_key[section_index], w_value[section_index], w_out[section_index], upstream, mask)
            outgoing.append(grad_x)
            stored.append(terms)
        grads_by_section[section_index] = section_weights(stored)
        inputs_by_section[section_index] = jnp.stack(outgoing)
        from_above = outgoing
    return (jnp.stack(grads_by_section), jnp.stack(inputs_by_section, axis=1))
```

```python
import functools
import math

import jax
import jax.numpy as jnp
from jax import lax
from jax.experimental import pallas as pl
from jax.experimental.pallas import tpu as pltpu
from jax.sharding import PartitionSpec as P

HEADS = 8
BLOCK = 128
ROWS = 256
WIDE = 1024
HEAD_DIM = 128
TILE = 256
STEPS = WIDE // TILE
EPSILON = 1e-06
SCALE = 1.0 / math.sqrt(HEAD_DIM)
PARTS = 32
UNLISTED = 3e38
BF = jnp.bfloat16
F32 = jnp.float32

AX, BX, AY, BY, ZZ = 8, 24, 1, 3, 4
ORDERS = (
    (AX, AY, BX, BY, ZZ),
    (BX, BY, AX, AY, ZZ),
    (AY, AX, BY, BX, ZZ),
    (BY, BX, AY, AX, ZZ),
)


def right_dot(left, right):
    return lax.dot_general(
        left, right, (((1,), (1,)), ((), ())), preferred_element_type=jnp.float32
    )


def left_dot(left, right):
    return lax.dot_general(
        left, right, (((0,), (0,)), ((), ())), preferred_element_type=jnp.float32
    )


def dot(left, right):
    return jnp.dot(left, right, preferred_element_type=jnp.float32)


def inverse_rms(x):
    return lax.rsqrt(jnp.mean(x * x, axis=-1, keepdims=True) + EPSILON)


def params():
    return pltpu.CompilerParams(
        dimension_semantics=("arbitrary",), vmem_limit_bytes=40 * 1024 * 1024
    )


def cost(flops, moved):
    return pl.CostEstimate(flops=int(flops), bytes_accessed=int(moved), transcendentals=0)


def shape(rows, columns, dtype=BF):
    return jax.ShapeDtypeStruct((rows, columns), dtype)


def whole(rows, columns=WIDE):
    return pl.BlockSpec((rows, columns), lambda i, info: (0, 0))


def part_of(rows, at=0):
    return pl.BlockSpec((rows, TILE), lambda i, info: (at, i))


def member_block(tick):
    return pl.BlockSpec((1, ROWS, WIDE), lambda i, info: (info[tick], 0, 0))


WEIGHT = pl.BlockSpec((WIDE, TILE), lambda i, info: (0, i))
WEIGHT_ROWS = pl.BlockSpec((TILE, WIDE), lambda i, info: (i, 0))


def call(kernel, info, args, in_specs, out_shape, out_specs, scratch, estimate, name):
    return pl.pallas_call(
        kernel,
        out_shape=out_shape,
        grid_spec=pltpu.PrefetchScalarGridSpec(
            num_scalar_prefetch=1,
            grid=(STEPS,),
            in_specs=in_specs,
            out_specs=out_specs,
            scratch_shapes=scratch,
        ),
        compiler_params=params(),
        cost_estimate=estimate,
        name=name,
    )(info, *args)


def project_kernel(info, xa, xb, wq, wk, wv, normed, q, k, v):
    rows = normed.shape[0] // 2

    @pl.when(pl.program_id(0) == 0)
    def _():
        for at, ref in enumerate((xa, xb)):
            x = (ref[0] if len(ref.shape) == 3 else ref[...]).astype(F32)
            normed[at * rows : (at + 1) * rows, :] = (x * inverse_rms(x)).astype(BF)

    n = normed[...]
    q[...] = dot(n, wq[...]).astype(BF)
    k[...] = dot(n, wk[...]).astype(BF)
    v[...] = dot(n, wv[...]).astype(BF)


def project(info, xs, x_specs, weights, name):
    rows = 2 * xs[0].shape[-2]
    return call(
        project_kernel,
        info,
        (*xs, *weights),
        [*x_specs, WEIGHT, WEIGHT, WEIGHT],
        [shape(rows, WIDE)] * 4,
        [whole(rows), part_of(rows), part_of(rows), part_of(rows)],
        [],
        cost(6 * rows * WIDE * WIDE, 6 * WIDE * WIDE + 10 * rows * WIDE),
        name,
    )


def attend_kernel(info, q, k, v, kh, vh, g, wo, att, dq, dk, dv, stats):
    step = pl.program_id(0)
    ga = right_dot(g[...], wo[...]).astype(BF)
    column = lax.broadcasted_iota(jnp.int32, (1, 3 * BLOCK), 1)
    lane = lax.broadcasted_iota(jnp.int32, (BLOCK, HEAD_DIM), 1)

    @pl.when(step == 0)
    def _():
        stats[...] = jnp.zeros_like(stats)

    valid = []
    listed = []
    for b in range(2):
        limit = [info[2 + 3 * b + e] for e in range(3)]
        inside = (column < limit[0]) & (column < BLOCK)
        for e in (1, 2):
            at = column - e * BLOCK
            inside = inside | ((at >= 0) & (at < limit[e]) & (at < BLOCK))
        valid.append(inside)
        listed.append(limit[2 * b] > 0)
    for hh in range(2):
        sl = slice(hh * HEAD_DIM, (hh + 1) * HEAD_DIM)
        head = step * 2 + hh
        kx = jnp.concatenate([kh[:BLOCK, sl], k[:, sl], kh[BLOCK:, sl]], axis=0)
        vx = jnp.concatenate([vh[:BLOCK, sl], v[:, sl], vh[BLOCK:, sl]], axis=0)
        dk_sum = None
        for b in range(2):
            rows = slice(b * BLOCK, (b + 1) * BLOCK)
            qb, gb = q[rows, sl], ga[rows, sl]
            kb, vb = kx[b * BLOCK : (b + 3) * BLOCK], vx[b * BLOCK : (b + 3) * BLOCK]
            s = jnp.where(valid[b], right_dot(qb, kb) * SCALE, -jnp.inf)
            peak = jnp.max(s, axis=-1, keepdims=True)
            raised = jnp.exp(s - peak)
            total = jnp.sum(raised, axis=-1, keepdims=True)
            p = raised * (1.0 / total)
            pb = p.astype(BF)
            att[rows, sl] = dot(pb, vb).astype(BF)
            gp = right_dot(gb, vb)
            mid = jnp.sum(p * gp, axis=-1, keepdims=True)
            ds = (p * (gp - mid) * SCALE).astype(BF)
            dq[rows, sl] = dot(ds, kb).astype(BF)
            own = slice(BLOCK, 3 * BLOCK) if b == 0 else slice(0, 2 * BLOCK)
            dk_now = left_dot(ds[:, own], qb)
            dv_now = left_dot(pb[:, own], gb)
            dk_sum, dv_sum = (
                (dk_now, dv_now) if dk_sum is None else (dk_sum + dk_now, dv_sum + dv_now)
            )
            sent_peak = jnp.where(listed[b], peak, UNLISTED)
            now = stats[rows, :]
            now = jnp.where(lane == head, sent_peak, now)
            now = jnp.where(lane == HEADS + head, total, now)
            stats[rows, :] = jnp.where(lane == 2 * HEADS + head, mid, now)
        dk[:, sl] = dk_sum
        dv[:, sl] = dv_sum


def attend(info, tick, q, k, v, kh, vh, g, wo):
    own = part_of(ROWS, tick)
    return call(
        attend_kernel,
        info,
        (q, k, v, kh, vh, g, wo),
        [own, own, own, part_of(ROWS), part_of(ROWS), whole(ROWS), WEIGHT_ROWS],
        [shape(ROWS, WIDE)] * 2 + [shape(ROWS, WIDE, F32)] * 2 + [shape(ROWS, HEAD_DIM, F32)],
        [part_of(ROWS)] * 4 + [whole(ROWS, HEAD_DIM)],
        [],
        cost(6 * 2 * ROWS * WIDE * WIDE, 12 * ROWS * WIDE * 2),
        f"attend{tick}",
    )


def finish_kernel(
    info, qh, g_prev, g_next, wo, k, v, s_prev, s_next, dq, dk, dv, wq, wk, wv, x, g, gk, gv, gx, gn
):
    step = pl.program_id(0)
    gah = right_dot(jnp.concatenate([g_prev[...], g_next[...]], axis=0), wo[...]).astype(BF)
    lane = lax.broadcasted_iota(jnp.int32, (BLOCK, HEAD_DIM), 1)
    column = lax.broadcasted_iota(jnp.int32, (1, BLOCK), 1)
    for hh in range(2):
        sl = slice(hh * HEAD_DIM, (hh + 1) * HEAD_DIM)
        head = step * 2 + hh
        for b, stats in enumerate((s_prev, s_next)):
            rows = slice(b * BLOCK, (b + 1) * BLOCK)

            def pick(at, stats=stats, head=head):
                chosen = jnp.where(lane == at * HEADS + head, stats[...], 0.0)
                return jnp.sum(chosen, axis=-1, keepdims=True)

            qb, kb, vb, gb = qh[rows, sl], k[rows, sl], v[rows, sl], gah[rows, sl]
            s = right_dot(qb, kb) * SCALE
            inside = column < info[3 + 3 * b]
            p = jnp.where(inside, jnp.exp(s - pick(0)), 0.0) * (1.0 / pick(1))
            ds = (p * (right_dot(gb, vb) - pick(2)) * SCALE).astype(BF)
            dk_far = left_dot(ds, qb).astype(BF).astype(F32)
            dv_far = left_dot(p.astype(BF), gb).astype(BF).astype(F32)
            gk[rows, sl] = (dk[rows, sl] + dk_far).astype(BF)
            gv[rows, sl] = (dv[rows, sl] + dv_far).astype(BF)
    now = (
        right_dot(dq[...], wq[...]) + right_dot(gk[...], wk[...]) + right_dot(gv[...], wv[...])
    )

    @pl.when(step == 0)
    def _():
        gn[...] = now

    @pl.when(step > 0)
    def _():
        gn[...] += now

    @pl.when(step == STEPS - 1)
    def _():
        xf = x[0].astype(F32)
        r = inverse_rms(xf)
        xr = xf * r
        grad = gn[...]
        grad_in = r * (grad - xr * jnp.mean(grad * xr, axis=-1, keepdims=True))
        gx[...] = (g[...].astype(F32) + grad_in).astype(BF)


def finish(info, tick, qh, g_edges, wo, k, v, stats, dq, dk, dv, weights, x, g):
    own, here = part_of(ROWS, tick), part_of(ROWS)
    edge, side = whole(BLOCK), whole(BLOCK, HEAD_DIM)
    return call(
        finish_kernel,
        info,
        (qh, *g_edges, wo, k, v, *stats, dq, dk, dv, *weights, x, g),
        [here, edge, edge, WEIGHT_ROWS, own, own, side, side, here, here, here]
        + [WEIGHT, WEIGHT, WEIGHT, member_block(tick), whole(ROWS)],
        [shape(ROWS, WIDE)] * 3,
        [here, here, whole(ROWS)],
        [pltpu.VMEM((ROWS, WIDE), F32)],
        cost(10 * ROWS * WIDE * WIDE, 8 * WIDE * WIDE + 20 * ROWS * WIDE),
        f"finish{tick}",
    )


def position(order, q):
    found = 0
    for bit, mask in enumerate(order):
        if (q >> (len(order) - 1 - bit)) & 1:
            found ^= mask
    return found


def weight_kernel(order, info, la, lb, ra, rb, keep, send, chunks):
    product = left_dot(la[...], ra[...]) + left_dot(lb[...], rb[...])
    chunks[...] = product.astype(BF).reshape(chunks.shape)
    me = info[8]
    half = PARTS // 2
    for q in range(PARTS):
        out = keep if q < half else send
        out[q % half] = chunks[lax.bitwise_xor(jnp.int32(position(order, q)), me)]


def weight_part(info, order, left, left_at, right, name):
    depth = WIDE // PARTS
    half = jax.ShapeDtypeStruct((PARTS // 2, depth, WIDE), BF)
    half_spec = pl.BlockSpec((PARTS // 2, depth, TILE), lambda i, info: (0, 0, i))

    def rows_at(at):
        return pl.BlockSpec((ROWS, WIDE), lambda i, info: (at, 0))

    return call(
        functools.partial(weight_kernel, order),
        info,
        (*left, *right),
        [rows_at(left_at[0]), rows_at(left_at[1]), part_of(ROWS), part_of(ROWS)],
        [half, half],
        [half_spec, half_spec],
        [pltpu.VMEM((PARTS, depth, TILE), BF)],
        cost(4 * ROWS * WIDE * WIDE, 8 * ROWS * WIDE + 2 * WIDE * WIDE),
        name,
    )


def swap(value, mask):
    return lax.ppermute(value, "mesh", [(p, p ^ mask) for p in range(PARTS)])


def add(left, right):
    return (left.astype(F32) + right.astype(F32)).astype(BF)


def ring(value, steps):
    return lax.ppermute(value, "mesh", [(p, (p + steps) % PARTS) for p in range(PARTS)])


def from_above(value, sections, steps):
    pairs = [
        (s * PARTS + p, (s - 1) * PARTS + (p + steps) % PARTS)
        for s in range(1, sections)
        for p in range(PARTS)
    ]
    return lax.ppermute(value, ("section", "mesh"), pairs)


def top_ring(value, sections, steps):
    base = (sections - 1) * PARTS
    pairs = [(base + p, base + (p + steps) % PARTS) for p in range(PARTS)]
    return lax.ppermute(value, ("section", "mesh"), pairs)


def per_device(
    saved_inputs, w_query, w_key, w_value, w_out, pending, top_grads, key_blocks, counts, plan
):
    sections = lax.axis_size("section")
    section_here = lax.axis_index("section")
    part_here = lax.axis_index("mesh")
    weights = (w_query[0], w_key[0], w_value[0])
    wo = w_out[0]
    saved = saved_inputs[0]
    members = lax.dynamic_slice_in_dim(plan, section_here, 1, axis=1)[:, 0]
    own_counts = lax.dynamic_slice_in_dim(counts, part_here * 2, 2)
    listed = jnp.where(key_blocks >= 0, counts[jnp.maximum(key_blocks, 0)], 0)
    limits = jnp.stack([listed[:, 1], own_counts, listed[:, 0]], axis=1)
    info = jnp.concatenate(
        [members, limits.reshape(6), part_here[None].astype(jnp.int32)]
    ).astype(jnp.int32)

    def edge(tick, at):
        return lax.dynamic_slice(
            saved, (members[tick], jnp.int32(at), jnp.int32(0)), (1, BLOCK, WIDE)
        )[0]

    g0 = pending[0]
    top = top_grads[0]
    last, first = ROWS - BLOCK, 0
    x_edges0 = (ring(edge(0, last), 1), ring(edge(0, first), -1))
    later = (edge(1, last), edge(1, first), g0[last:], g0[:BLOCK], top[last:], top[:BLOCK])
    x_edges0, later = lax.optimization_barrier((x_edges0, later))
    g_edges0 = (ring(later[2], 1), ring(later[3], -1))
    x_edges1 = (ring(later[0], 1), ring(later[1], -1))
    top_edges = (top_ring(later[4], sections, 1), top_ring(later[5], sections, -1))

    normed, q, k, v = project(
        info, (saved, saved), (member_block(0), member_block(1)), weights, "project_own"
    )
    is_top = section_here == sections - 1
    g, g_edges = g0, g_edges0
    outgoing, attended, grads = [], [], []
    for tick in range(2):
        x_edges = (x_edges0, x_edges1)[tick]
        _, qh, kh, vh = project(
            info, x_edges, (whole(BLOCK), whole(BLOCK)), weights, f"project_edge{tick}"
        )
        if tick == 1:
            grad_x = outgoing[0]
            passed = from_above(grad_x, sections, 0)
            passed_prev = from_above(grad_x[last:], sections, 1)
            passed_next = from_above(grad_x[:BLOCK], sections, -1)
            g = jnp.where(is_top, top, passed)
            g_edges = (
                jnp.where(is_top, top_edges[0], passed_prev),
                jnp.where(is_top, top_edges[1], passed_next),
            )
        att, dq, dk, dv, stats = attend(info, tick, q, k, v, kh, vh, g, wo)
        far = (ring(stats[BLOCK:], 1), ring(stats[:BLOCK], -1))
        gk, gv, gx = finish(
            info, tick, qh, g_edges, wo, k, v, far, dq, dk, dv, weights, saved, g
        )
        outgoing.append(gx)
        attended.append(att)
        grads.append((dq, gk, gv, g))

    sums = []
    for w in (3, 0, 1, 2):
        left = attended if w == 3 else (normed, normed)
        left_at = (0, 0) if w == 3 else (0, 1)
        right = (grads[0][w], grads[1][w])
        keep, send = weight_part(info, ORDERS[w], left, left_at, right, f"weight{w}")
        sums.append((w, keep, send))
    for stage in range(4):
        following = []
        for w, keep, send in sums:
            received = swap(send, ORDERS[w][stage])
            half = keep.shape[0] // 2
            following.append(
                (w, add(keep[:half], received[:half]), add(keep[half:], received[half:]))
            )
        sums = following
    sums.sort(key=lambda item: item[0])
    kept = jnp.stack([item[1][0] for item in sums], axis=1)
    sent = jnp.stack([item[2][0] for item in sums], axis=1)
    layer_total = kept.astype(F32) + swap(sent, ZZ).astype(F32)
    return (layer_total[None], jnp.stack(outgoing)[:, None])


def solution(mesh):
    in_specs = (
        P("section", None, "mesh", None),
        P("section", None, None),
        P("section", None, None),
        P("section", None, None),
        P("section", None, None),
        P("section", "mesh", None),
        P(None, "mesh", None),
        P("mesh", None),
        P(),
        P(),
    )
    out_specs = (P("section", "mesh", None, None), P(None, "section", "mesh", None))
    return jax.shard_map(
        per_device, mesh=mesh, in_specs=in_specs, out_specs=out_specs, check_vma=False
    )
```

```python
import functools
import math

import jax
import jax.numpy as jnp
from jax import lax
from jax.experimental import pallas as pl
from jax.experimental.pallas import tpu as pltpu
from jax.sharding import PartitionSpec as P

HEADS = 8
BLOCK = 128
ROWS = 256
WIDE = 1024
HEAD_DIM = 128
SECTIONS = 8
VMEM_LIMIT = 24 * 1024 * 1024
EPSILON = 1e-06
SCALE = 1.0 / math.sqrt(HEAD_DIM)
PARTS = 32
UNLISTED = 3e38
BF = jnp.bfloat16
F32 = jnp.float32

AX, BX, AY, BY, ZZ = 8, 24, 1, 3, 4
ORDERS = (
    (AX, AY, BX, BY, ZZ),
    (BX, BY, AX, AY, ZZ),
    (AY, AX, BY, BX, ZZ),
    (BY, BX, AY, AX, ZZ),
)


def right_dot(left, right):
    return lax.dot_general(
        left, right, (((1,), (1,)), ((), ())), preferred_element_type=jnp.float32
    )


def left_dot(left, right):
    return lax.dot_general(
        left, right, (((0,), (0,)), ((), ())), preferred_element_type=jnp.float32
    )


def dot(left, right):
    return jnp.dot(left, right, preferred_element_type=jnp.float32)


def inverse_rms(x):
    return lax.rsqrt(jnp.mean(x * x, axis=-1, keepdims=True) + EPSILON)


def cost(flops, moved):
    return pl.CostEstimate(flops=int(flops), bytes_accessed=int(moved), transcendentals=0)


def shape(rows, columns, dtype=BF):
    return jax.ShapeDtypeStruct((rows, columns), dtype)


def space(value):
    return pltpu.SMEM if value.dtype == jnp.int32 else pltpu.VMEM


def call(kernel, args, out_shape, scratch, estimate, name):
    return pl.pallas_call(
        kernel,
        out_shape=out_shape,
        in_specs=[pl.BlockSpec(memory_space=space(value)) for value in args],
        out_specs=[pl.BlockSpec(memory_space=space(value)) for value in out_shape],
        scratch_shapes=scratch,
        compiler_params=pltpu.CompilerParams(vmem_limit_bytes=VMEM_LIMIT),
        cost_estimate=estimate,
        name=name,
    )(*args)


def prepare_kernel(ids, plan, counts, key_blocks, saved, pending, info, *rest):
    outs, sems = rest[:-1], rest[-1]
    section, part = ids[0], ids[1]
    first, last = slice(0, BLOCK), slice(ROWS - BLOCK, ROWS)
    members = [plan[tick, section] for tick in range(2)]
    sources = (
        saved.at[members[0], last],
        saved.at[members[0], first],
        pending.at[last],
        pending.at[first],
        saved.at[members[1], last],
        saved.at[members[1], first],
        saved.at[members[0]],
        saved.at[members[1]],
    )
    copies = [
        pltpu.make_async_copy(source, out, sems.at[n])
        for n, (source, out) in enumerate(zip(sources, outs))
    ]
    for copy in copies:
        copy.start()
    info[0] = part
    info[1] = section
    for b in range(2):
        for e, j in ((0, 1), (2, 0)):
            listed = key_blocks[b, j]
            found = counts[jnp.maximum(listed, 0)]
            info[2 + 3 * b + e] = jnp.where(listed >= 0, found, 0)
        info[3 + 3 * b] = counts[part * 2 + b]
    for copy in copies:
        copy.wait()


def prepare(ids, plan, counts, key_blocks, saved, pending):
    smem = pl.BlockSpec(memory_space=pltpu.SMEM)
    anywhere = pl.BlockSpec(memory_space=pl.ANY)
    return pl.pallas_call(
        prepare_kernel,
        out_shape=[jax.ShapeDtypeStruct((8,), jnp.int32)]
        + [shape(BLOCK, WIDE)] * 6
        + [shape(ROWS, WIDE)] * 2,
        in_specs=[smem] * 4 + [anywhere] * 2,
        out_specs=[smem] + [anywhere] * 8,
        scratch_shapes=[pltpu.SemaphoreType.DMA((8,))],
        compiler_params=pltpu.CompilerParams(vmem_limit_bytes=VMEM_LIMIT),
        name="prepare",
    )(ids, plan, counts, key_blocks, saved, pending)


def project_kernel(keep_normed, xa, xb, wq, wk, wv, *outs):
    parts = []
    for ref in (xa, xb):
        x = ref[...].astype(F32)
        parts.append((x * inverse_rms(x)).astype(BF))
    normed = jnp.concatenate(parts, axis=0)
    if keep_normed:
        outs[0][...] = normed
    for weight, out in zip((wq, wk, wv), outs[-3:]):
        out[...] = dot(normed, weight[...]).astype(BF)


def project(xs, weights, keep_normed, name):
    rows = 2 * xs[0].shape[0]
    return call(
        functools.partial(project_kernel, keep_normed),
        (*xs, *weights),
        [shape(rows, WIDE)] * (3 + keep_normed),
        [],
        cost(6 * rows * WIDE * WIDE, 6 * WIDE * WIDE + 10 * rows * WIDE),
        name,
    )


def attend_kernel(tick, info, q, k, v, kh, vh, wo, *rest):
    if tick == 0:
        g, att, dq, dk, dv, stats_first, stats_last = rest
        upstream = g[...]
    else:
        g, top, att, dq, dk, dv, stats_first, stats_last, upstream_out = rest
        upstream = jnp.where(info[1] == SECTIONS - 1, top[...], g[...])
        upstream_out[...] = upstream
    ga = right_dot(upstream, wo[...]).astype(BF)
    place = lax.broadcasted_iota(jnp.int32, (3 * BLOCK, 1), 0)
    base = tick * ROWS
    valid = []
    listed = []
    for b in range(2):
        limit = [info[2 + 3 * b + e] for e in range(3)]
        inside = place < jnp.minimum(limit[0], BLOCK)
        for e in (1, 2):
            at = place - e * BLOCK
            inside = inside | ((at >= 0) & (at < jnp.minimum(limit[e], BLOCK)))
        valid.append(inside)
        listed.append(limit[2 * b] > 0)
    for head in range(HEADS):
        sl = slice(head * HEAD_DIM, (head + 1) * HEAD_DIM)
        kx = jnp.concatenate([kh[:BLOCK, sl], k[base : base + ROWS, sl], kh[BLOCK:, sl]], axis=0)
        vx = jnp.concatenate([vh[:BLOCK, sl], v[base : base + ROWS, sl], vh[BLOCK:, sl]], axis=0)
        dk_sum = None
        for b in range(2):
            rows = slice(b * BLOCK, (b + 1) * BLOCK)
            qb, gb = q[base + b * BLOCK : base + (b + 1) * BLOCK, sl], ga[rows, sl]
            kb, vb = kx[b * BLOCK : (b + 3) * BLOCK], vx[b * BLOCK : (b + 3) * BLOCK]
            s = jnp.where(valid[b], right_dot(kb, qb) * SCALE, -jnp.inf)
            peak = jnp.max(s, axis=0, keepdims=True)
            raised = jnp.exp(s - peak)
            total = jnp.sum(raised, axis=0, keepdims=True)
            p = raised * (1.0 / total)
            pb = p.astype(BF)
            att[rows, sl] = left_dot(pb, vb).astype(BF)
            gp = right_dot(vb, gb)
            mid = jnp.sum(p * gp, axis=0, keepdims=True)
            ds = (p * (gp - mid) * SCALE).astype(BF)
            dq[rows, sl] = left_dot(ds, kb).astype(BF)
            own = slice(BLOCK, 3 * BLOCK) if b == 0 else slice(0, 2 * BLOCK)
            dk_now = dot(ds[own], qb)
            dv_now = dot(pb[own], gb)
            dk_sum, dv_sum = (
                (dk_now, dv_now) if dk_sum is None else (dk_sum + dk_now, dv_sum + dv_now)
            )
            stats = (stats_first, stats_last)[b]
            stats[head : head + 1, :] = jnp.where(listed[b], peak, UNLISTED)
            stats[HEADS + head : HEADS + head + 1, :] = total
            stats[2 * HEADS + head : 2 * HEADS + head + 1, :] = mid
        dk[:, sl] = dk_sum
        dv[:, sl] = dv_sum


def attend(info, tick, q, k, v, kh, vh, wo, upstream):
    outs = [shape(ROWS, WIDE)] * 2 + [shape(ROWS, WIDE, F32)] * 2
    outs += [shape(3 * HEADS, BLOCK, F32)] * 2 + [shape(ROWS, WIDE)] * tick
    return call(
        functools.partial(attend_kernel, tick),
        (info, q, k, v, kh, vh, wo, *upstream),
        outs,
        [],
        cost(8 * 2 * ROWS * WIDE * WIDE, 12 * ROWS * WIDE * 2),
        f"attend{tick}",
    )


def finish_kernel(tick, info, qh, g_prev, g_next, wo, k, v, s_prev, s_next, dq, dk, dv, *rest):
    if tick == 0:
        wq, wk, wv, x, g, top, gk, gv, gx, edge_last, edge_first = rest
    else:
        wq, wk, wv, x, g, gk, gv, gx = rest
    base = tick * ROWS
    gah = right_dot(jnp.concatenate([g_prev[...], g_next[...]], axis=0), wo[...]).astype(BF)
    place = lax.broadcasted_iota(jnp.int32, (BLOCK, 1), 0)
    for head in range(HEADS):
        sl = slice(head * HEAD_DIM, (head + 1) * HEAD_DIM)
        for b, stats in enumerate((s_prev, s_next)):
            rows = slice(b * BLOCK, (b + 1) * BLOCK)
            mine = slice(base + b * BLOCK, base + (b + 1) * BLOCK)
            peak, total, mid = (
                stats[at * HEADS + head : at * HEADS + head + 1, :] for at in range(3)
            )
            qb, kb, vb, gb = qh[rows, sl], k[mine, sl], v[mine, sl], gah[rows, sl]
            s = right_dot(kb, qb) * SCALE
            inside = place < info[3 + 3 * b]
            p = jnp.where(inside, jnp.exp(s - peak), 0.0) * (1.0 / total)
            ds = (p * (right_dot(vb, gb) - mid) * SCALE).astype(BF)
            dk_far = dot(ds, qb).astype(BF).astype(F32)
            dv_far = dot(p.astype(BF), gb).astype(BF).astype(F32)
            gk[rows, sl] = (dk[rows, sl] + dk_far).astype(BF)
            gv[rows, sl] = (dv[rows, sl] + dv_far).astype(BF)
    grad = (
        right_dot(dq[...], wq[...]) + right_dot(gk[...], wk[...]) + right_dot(gv[...], wv[...])
    )
    xf = x[...].astype(F32)
    r = inverse_rms(xf)
    xr = xf * r
    grad_in = r * (grad - xr * jnp.mean(grad * xr, axis=-1, keepdims=True))
    out = (g[...].astype(F32) + grad_in).astype(BF)
    gx[...] = out
    if tick == 0:
        at_bottom = info[1] == 0
        edge_last[...] = jnp.where(at_bottom, top[BLOCK:, :], out[BLOCK:, :])
        edge_first[...] = jnp.where(at_bottom, top[:BLOCK, :], out[:BLOCK, :])


def finish(info, tick, qh, g_edges, wo, k, v, stats, dq, dk, dv, weights, x, gs):
    edges = [shape(BLOCK, WIDE)] * (2 - 2 * tick)
    return call(
        functools.partial(finish_kernel, tick),
        (info, qh, *g_edges, wo, k, v, *stats, dq, dk, dv, *weights, x, *gs),
        [shape(ROWS, WIDE)] * 3 + edges,
        [],
        cost(10 * ROWS * WIDE * WIDE, 8 * WIDE * WIDE + 20 * ROWS * WIDE),
        f"finish{tick}",
    )


def position(order, q):
    found = 0
    for bit, mask in enumerate(order):
        if (q >> (len(order) - 1 - bit)) & 1:
            found ^= mask
    return found


def weight_kernel(order, offset, info, la, lb, ra, rb, keep, send, chunks):
    product = left_dot(la[:ROWS, :], ra[...]) + left_dot(lb[offset : offset + ROWS, :], rb[...])
    chunks[...] = product.astype(BF).reshape(chunks.shape)
    me = info[0]
    half = PARTS // 2
    for q in range(PARTS):
        out = keep if q < half else send
        out[q % half] = chunks[lax.bitwise_xor(jnp.int32(position(order, q)), me)]


def weight_part(info, order, left, offset, right, name):
    depth = WIDE // PARTS
    half = jax.ShapeDtypeStruct((PARTS // 2, depth, WIDE), BF)
    return call(
        functools.partial(weight_kernel, order, offset),
        (info, *left, *right),
        [half, half],
        [pltpu.VMEM((PARTS, depth, WIDE), BF)],
        cost(4 * ROWS * WIDE * WIDE, 8 * ROWS * WIDE + 2 * WIDE * WIDE),
        name,
    )


def swap(value, mask):
    return lax.ppermute(value, "mesh", [(p, p ^ mask) for p in range(PARTS)])


def add(left, right):
    return (left.astype(F32) + right.astype(F32)).astype(BF)


def ring(value, steps):
    return lax.ppermute(value, "mesh", [(p, (p + steps) % PARTS) for p in range(PARTS)])


def from_above(value, sections, steps, cyclic):
    pairs = [
        (s * PARTS + p, (s - 1) % sections * PARTS + (p + steps) % PARTS)
        for s in range(0 if cyclic else 1, sections)
        for p in range(PARTS)
    ]
    return lax.ppermute(value, ("section", "mesh"), pairs)


def halve(parts, first, last):
    for stage in range(first, last):
        following = []
        for w, keep, send in parts:
            received = swap(send, ORDERS[w][stage])
            half = keep.shape[0] // 2
            following.append(
                (w, add(keep[:half], received[:half]), add(keep[half:], received[half:]))
            )
        parts = following
    return parts


def per_device(
    saved_inputs, w_query, w_key, w_value, w_out, pending, top_grads, key_blocks, counts, plan
):
    sections = lax.axis_size("section")
    ids = jnp.stack([lax.axis_index("section"), lax.axis_index("mesh")]).astype(jnp.int32)
    weights = (w_query[0], w_key[0], w_value[0])
    wo = w_out[0]
    g0, top = pending[0], top_grads[0]
    info, last0, first0, g_last, g_first, last1, first1, x0, x1 = prepare(
        ids, plan, counts, key_blocks, saved_inputs[0], g0
    )
    x_edges0 = (ring(last0, 1), ring(first0, -1))
    normed, q, k, v = project((x0, x1), weights, True, "project_own")
    (g_last, g_first), q = lax.optimization_barrier(((g_last, g_first), q))
    g_edges0 = (ring(g_last, 1), ring(g_first, -1))
    qh, kh, vh = project(x_edges0, weights, False, "project_edge0")
    att0, dq0, dk, dv, stats_first, stats_last = attend(info, 0, q, k, v, kh, vh, wo, (g0,))
    stats = (ring(stats_last, 1), ring(stats_first, -1))
    (last1, first1), stats_last = lax.optimization_barrier(((last1, first1), stats_last))
    x_edges1 = (ring(last1, 1), ring(first1, -1))
    gk0, gv0, gx0, edge_last, edge_first = finish(
        info, 0, qh, g_edges0, wo, k, v, stats, dq0, dk, dv, weights, x0, (g0, top)
    )
    passed = from_above(gx0, sections, 0, False)
    g_edges1 = (
        from_above(edge_last, sections, 1, True),
        from_above(edge_first, sections, -1, True),
    )
    qh, kh, vh = project(x_edges1, weights, False, "project_edge1")
    att1, dq1, dk, dv, stats_first, stats_last, g1 = attend(
        info, 1, q, k, v, kh, vh, wo, (passed, top)
    )
    stats = (ring(stats_last, 1), ring(stats_first, -1))
    early = []
    for w, left, right in ((3, (att0, att1), (g0, g1)), (0, (normed, normed), (dq0, dq1))):
        offset = 0 if w == 3 else ROWS
        early.append((w, *weight_part(info, ORDERS[w], left, offset, right, f"weight{w}")))
    gk1, gv1, gx1 = finish(
        info, 1, qh, g_edges1, wo, k, v, stats, dq1, dk, dv, weights, x1, (g1,)
    )
    late = []
    for w, right in ((1, (gk0, gk1)), (2, (gv0, gv1))):
        late.append(
            (w, *weight_part(info, ORDERS[w], (normed, normed), ROWS, right, f"weight{w}"))
        )
    totals = {}
    for group in (early, late):
        done = halve(group, 0, 4)
        received = swap(jnp.stack([send[0] for _, _, send in done]), ZZ)
        for at, (w, keep, _) in enumerate(done):
            totals[w] = keep[0].astype(F32) + received[at].astype(F32)
    layer_total = jnp.stack([totals[w] for w in range(4)], axis=1)
    return (layer_total[None], jnp.stack([gx0, gx1])[:, None])


def solution(mesh):
    in_specs = (
        P("section", None, "mesh", None),
        P("section", None, None),
        P("section", None, None),
        P("section", None, None),
        P("section", None, None),
        P("section", "mesh", None),
        P(None, "mesh", None),
        P("mesh", None),
        P(),
        P(),
    )
    out_specs = (P("section", "mesh", None, None), P(None, "section", "mesh", None))
    return jax.shard_map(
        per_device, mesh=mesh, in_specs=in_specs, out_specs=out_specs, check_vma=False
    )
```

```python
import functools
import math

import jax
import jax.numpy as jnp
from jax import lax
from jax.experimental import pallas as pl
from jax.experimental.pallas import tpu as pltpu
from jax.sharding import PartitionSpec as P

HEADS = 8
BLOCK = 128
ROWS = 256
WIDE = 1024
HEAD_DIM = 128
SECTIONS = 8
VMEM_LIMIT = 16 * 1024 * 1024
EPSILON = 1e-06
SCALE = 1.0 / math.sqrt(HEAD_DIM)
PARTS = 32
UNLISTED = 3e38
BF = jnp.bfloat16
F32 = jnp.float32

AX, BX, AY, BY, ZZ = 8, 24, 1, 3, 4
EARLY_ORDERS = (
    ((AX, AY, BX, BY, ZZ), (AY, AX, BX, BY, ZZ)),
    ((BX, BY, AX, AY, ZZ), (BY, BX, AX, AY, ZZ)),
)
LATE_ORDERS = (
    ((AX, AY, BY, BX, ZZ), (AY, AX, BY, BX, ZZ)),
    ((BX, BY, AY, AX, ZZ), (BY, BX, AY, AX, ZZ)),
)
DEPTH = WIDE // PARTS


def right_dot(left, right):
    return lax.dot_general(
        left, right, (((1,), (1,)), ((), ())), preferred_element_type=jnp.float32
    )


def left_dot(left, right):
    return lax.dot_general(
        left, right, (((0,), (0,)), ((), ())), preferred_element_type=jnp.float32
    )


def dot(left, right):
    return jnp.dot(left, right, preferred_element_type=jnp.float32)


def inverse_rms(x):
    return lax.rsqrt(jnp.mean(x * x, axis=-1, keepdims=True) + EPSILON)


def cost(flops, moved):
    return pl.CostEstimate(flops=int(flops), bytes_accessed=int(moved), transcendentals=0)


def shape(rows, columns, dtype=BF):
    return jax.ShapeDtypeStruct((rows, columns), dtype)


def space(value):
    return pltpu.SMEM if value.dtype == jnp.int32 else pltpu.VMEM


def call(kernel, args, out_shape, scratch, estimate, name):
    return pl.pallas_call(
        kernel,
        out_shape=out_shape,
        in_specs=[pl.BlockSpec(memory_space=space(value)) for value in args],
        out_specs=[pl.BlockSpec(memory_space=space(value)) for value in out_shape],
        scratch_shapes=scratch,
        compiler_params=pltpu.CompilerParams(vmem_limit_bytes=VMEM_LIMIT),
        cost_estimate=estimate,
        name=name,
    )(*args)


def prepare_kernel(block_count, ints, saved, info, edge_last, edge_first, x0, x1):
    section, part = ints[0], ints[1]
    plan_at, counts_at, sections = 2, 2 + 2 * SECTIONS, SECTIONS
    blocks_at = counts_at + block_count
    first, last = slice(0, BLOCK), slice(ROWS - BLOCK, ROWS)
    m0, m1 = ints[plan_at + section], ints[plan_at + sections + section]
    edge_last[...] = saved[m0, last]
    edge_first[...] = saved[m0, first]
    x0[...] = saved[m0]
    x1[...] = saved[m1]
    info[0] = part
    info[1] = section
    for b in range(2):
        for e, j in ((0, 1), (2, 0)):
            listed = ints[blocks_at + 2 * b + j]
            found = ints[counts_at + jnp.maximum(listed, 0)]
            info[2 + 3 * b + e] = jnp.where(listed >= 0, found, 0)
        info[3 + 3 * b] = ints[counts_at + part * 2 + b]


def prepare(ids, plan, counts, key_blocks, saved):
    ints = jnp.concatenate([ids, plan.reshape(-1), counts, key_blocks.reshape(-1)])
    return call(
        functools.partial(prepare_kernel, counts.shape[0]),
        (ints, saved),
        [jax.ShapeDtypeStruct((8,), jnp.int32)]
        + [shape(BLOCK, WIDE)] * 2
        + [shape(ROWS, WIDE)] * 2,
        [],
        cost(0, 6 * ROWS * WIDE * 2),
        "prepare",
    )


def normalised(x):
    x = x.astype(F32)
    return (x * inverse_rms(x)).astype(BF)


def project_own_kernel(xa, xb, g, wq, wk, wv, normed_out, q, k, v, later_last, later_first):
    normed = jnp.concatenate([normalised(xa[...]), normalised(xb[...])], axis=0)
    normed_out[...] = normed
    for rows, later in ((slice(ROWS - BLOCK, ROWS), later_last), (slice(0, BLOCK), later_first)):
        later[:BLOCK, :] = g[rows, :]
        later[BLOCK:, :] = xb[rows, :]
    for weight, out in ((wq, q), (wk, k), (wv, v)):
        out[...] = dot(normed, weight[...]).astype(BF)


def project_own(xs, g, weights):
    rows = 2 * ROWS
    return call(
        project_own_kernel,
        (*xs, g, *weights),
        [shape(rows, WIDE)] * 4 + [shape(ROWS, WIDE)] * 2,
        [],
        cost(6 * rows * WIDE * WIDE, 6 * WIDE * WIDE + 10 * rows * WIDE),
        "project_own",
    )


def project_edge_kernel(xa, xb, wq, wk, wv, q, k, v):
    parts = [normalised(ref[ref.shape[0] - BLOCK :, :]) for ref in (xa, xb)]
    normed = jnp.concatenate(parts, axis=0)
    for weight, out in ((wq, q), (wk, k), (wv, v)):
        out[...] = dot(normed, weight[...]).astype(BF)


def project_edge(xs, weights, name):
    return call(
        project_edge_kernel,
        (*xs, *weights),
        [shape(ROWS, WIDE)] * 3,
        [],
        cost(6 * ROWS * WIDE * WIDE, 6 * WIDE * WIDE + 10 * ROWS * WIDE),
        name,
    )


def attend_kernel(tick, info, q, k, v, kh, vh, wo, *rest):
    if tick == 0:
        g, att, dq, dk, dv, stats_first, stats_last = rest
        upstream = g[...]
    else:
        g, top, att, dq, dk, dv, stats_first, stats_last, upstream_out = rest
        upstream = jnp.where(info[1] == SECTIONS - 1, top[...], g[...])
        upstream_out[...] = upstream
    ga = right_dot(upstream, wo[...]).astype(BF)
    place = lax.broadcasted_iota(jnp.int32, (3 * BLOCK, 1), 0)
    base = tick * ROWS
    valid = []
    listed = []
    for b in range(2):
        limit = [info[2 + 3 * b + e] for e in range(3)]
        inside = place < jnp.minimum(limit[0], BLOCK)
        for e in (1, 2):
            at = place - e * BLOCK
            inside = inside | ((at >= 0) & (at < jnp.minimum(limit[e], BLOCK)))
        valid.append(inside)
        listed.append(limit[2 * b] > 0)
    for head in range(HEADS):
        sl = slice(head * HEAD_DIM, (head + 1) * HEAD_DIM)
        kx = jnp.concatenate([kh[:BLOCK, sl], k[base : base + ROWS, sl], kh[BLOCK:, sl]], axis=0)
        vx = jnp.concatenate([vh[:BLOCK, sl], v[base : base + ROWS, sl], vh[BLOCK:, sl]], axis=0)
        dk_sum = None
        for b in range(2):
            rows = slice(b * BLOCK, (b + 1) * BLOCK)
            qb, gb = q[base + b * BLOCK : base + (b + 1) * BLOCK, sl], ga[rows, sl]
            kb, vb = kx[b * BLOCK : (b + 3) * BLOCK], vx[b * BLOCK : (b + 3) * BLOCK]
            s = jnp.where(valid[b], right_dot(kb, qb) * SCALE, -jnp.inf)
            peak = jnp.max(s, axis=0, keepdims=True)
            raised = jnp.exp(s - peak)
            total = jnp.sum(raised, axis=0, keepdims=True)
            p = raised * (1.0 / total)
            pb = p.astype(BF)
            att[rows, sl] = left_dot(pb, vb).astype(BF)
            gp = right_dot(vb, gb)
            mid = jnp.sum(p * gp, axis=0, keepdims=True)
            ds = (p * (gp - mid) * SCALE).astype(BF)
            dq[rows, sl] = left_dot(ds, kb).astype(BF)
            own = slice(BLOCK, 3 * BLOCK) if b == 0 else slice(0, 2 * BLOCK)
            dk_now = dot(ds[own], qb)
            dv_now = dot(pb[own], gb)
            dk_sum, dv_sum = (
                (dk_now, dv_now) if dk_sum is None else (dk_sum + dk_now, dv_sum + dv_now)
            )
            stats = (stats_first, stats_last)[b]
            stats[head : head + 1, :] = jnp.where(listed[b], peak, UNLISTED)
            stats[HEADS + head : HEADS + head + 1, :] = total
            stats[2 * HEADS + head : 2 * HEADS + head + 1, :] = mid
        dk[:, sl] = dk_sum
        dv[:, sl] = dv_sum


def attend(info, tick, q, k, v, kh, vh, wo, upstream):
    outs = [shape(ROWS, WIDE)] * 2 + [shape(ROWS, WIDE, F32)] * 2
    outs += [shape(3 * HEADS, BLOCK, F32)] * 2 + [shape(ROWS, WIDE)] * tick
    return call(
        functools.partial(attend_kernel, tick),
        (info, q, k, v, kh, vh, wo, *upstream),
        outs,
        [],
        cost(8 * 2 * ROWS * WIDE * WIDE, 12 * ROWS * WIDE * 2),
        f"attend{tick}",
    )


def ahead_kernel(g_prev, g_next, wo, dq, wq, gah, part):
    g_far = jnp.concatenate([g_prev[:BLOCK, :], g_next[:BLOCK, :]], axis=0)
    gah[...] = right_dot(g_far, wo[...]).astype(BF)
    part[...] = right_dot(dq[...], wq[...])


def ahead(g_edges, wo, dq, wq, name):
    return call(
        ahead_kernel,
        (*g_edges, wo, dq, wq),
        [shape(ROWS, WIDE), shape(ROWS, WIDE, F32)],
        [],
        cost(4 * ROWS * WIDE * WIDE, 4 * WIDE * WIDE + 8 * ROWS * WIDE),
        name,
    )


def cross_kernel(tick, info, qh, gah, k, v, s_prev, s_next, dk, dv, gk, gv):
    base = tick * ROWS
    place = lax.broadcasted_iota(jnp.int32, (BLOCK, 1), 0)
    for head in range(HEADS):
        sl = slice(head * HEAD_DIM, (head + 1) * HEAD_DIM)
        for b, stats in enumerate((s_prev, s_next)):
            rows = slice(b * BLOCK, (b + 1) * BLOCK)
            mine = slice(base + b * BLOCK, base + (b + 1) * BLOCK)
            peak, total, mid = (
                stats[at * HEADS + head : at * HEADS + head + 1, :] for at in range(3)
            )
            qb, kb, vb, gb = qh[rows, sl], k[mine, sl], v[mine, sl], gah[rows, sl]
            s = right_dot(kb, qb) * SCALE
            inside = place < info[3 + 3 * b]
            p = jnp.where(inside, jnp.exp(s - peak), 0.0) * (1.0 / total)
            ds = (p * (right_dot(vb, gb) - mid) * SCALE).astype(BF)
            dk_far = dot(ds, qb).astype(BF).astype(F32)
            dv_far = dot(p.astype(BF), gb).astype(BF).astype(F32)
            gk[rows, sl] = (dk[rows, sl] + dk_far).astype(BF)
            gv[rows, sl] = (dv[rows, sl] + dv_far).astype(BF)


def cross(info, tick, qh, gah, k, v, stats, dk, dv):
    return call(
        functools.partial(cross_kernel, tick),
        (info, qh, gah, k, v, *stats, dk, dv),
        [shape(ROWS, WIDE)] * 2,
        [],
        cost(2 * ROWS * WIDE * WIDE, 20 * ROWS * WIDE),
        f"cross{tick}",
    )


def grad_kernel(tick, info, part, gk, gv, wk, wv, x, g, *rest):
    gx = rest[0] if tick else rest[1]
    grad = part[...] + right_dot(gk[...], wk[...]) + right_dot(gv[...], wv[...])
    xf = x[...].astype(F32)
    r = inverse_rms(xf)
    xr = xf * r
    grad_in = r * (grad - xr * jnp.mean(grad * xr, axis=-1, keepdims=True))
    out = (g[...].astype(F32) + grad_in).astype(BF)
    gx[...] = out
    if tick == 0:
        top, _, edge_last, edge_first = rest
        at_bottom = info[1] == 0
        edge_last[...] = jnp.where(at_bottom, top[BLOCK:, :], out[BLOCK:, :])
        edge_first[...] = jnp.where(at_bottom, top[:BLOCK, :], out[:BLOCK, :])


def grad(info, tick, part, gk, gv, weights, x, gs):
    edges = [shape(BLOCK, WIDE)] * (2 - 2 * tick)
    return call(
        functools.partial(grad_kernel, tick),
        (info, part, gk, gv, *weights[1:], x, *gs),
        [shape(ROWS, WIDE)] + edges,
        [],
        cost(4 * ROWS * WIDE * WIDE, 4 * WIDE * WIDE + 12 * ROWS * WIDE),
        f"grad{tick}",
    )


def position(order, q):
    found = 0
    for bit, mask in enumerate(order):
        if (q >> (len(order) - 1 - bit)) & 1:
            found ^= mask
    return found


def weight_kernel(orders, offset, info, la, lb, ra, rb, *outs):
    chunks = outs[-1]
    product = left_dot(la[:ROWS, :], ra[...]) + left_dot(lb[offset : offset + ROWS, :], rb[...])
    chunks[...] = product.astype(BF).reshape(chunks.shape)
    me = info[0]
    half, wide = PARTS // 2, WIDE // len(orders)
    for n, order in enumerate(orders):
        columns = slice(n * wide, (n + 1) * wide)
        for q in range(PARTS):
            at = lax.bitwise_xor(jnp.int32(position(order, q)), me)
            outs[2 * n + q // half][q % half] = chunks[at, :, columns]


def weight_part(info, orders, left, offset, right, name):
    half = jax.ShapeDtypeStruct((PARTS // 2, DEPTH, WIDE // len(orders)), BF)
    return call(
        functools.partial(weight_kernel, orders, offset),
        (info, *left, *right),
        [half] * (2 * len(orders)),
        [pltpu.VMEM((PARTS, DEPTH, WIDE), BF)],
        cost(4 * ROWS * WIDE * WIDE, 8 * ROWS * WIDE + 2 * WIDE * WIDE),
        name,
    )


def merge_kernel(ka, ra, kb, rb, keep, send):
    half = keep.shape[0]
    for n, (kept, got) in enumerate(((ka, ra), (kb, rb))):
        columns = slice(n * WIDE // 2, (n + 1) * WIDE // 2)
        total = (kept[...].astype(F32) + got[...].astype(F32)).astype(BF)
        keep[:, :, columns] = total[:half]
        send[:, :, columns] = total[half:]


def merge(ka, ra, kb, rb, name):
    half = jax.ShapeDtypeStruct((ka.shape[0] // 2, DEPTH, WIDE), BF)
    return call(
        merge_kernel, (ka, ra, kb, rb), [half] * 2, [], cost(ka.size, 8 * ka.size), name
    )


def swap(value, mask):
    return lax.ppermute(value, "mesh", [(p, p ^ mask) for p in range(PARTS)])


def add(left, right):
    return (left.astype(F32) + right.astype(F32)).astype(BF)


def ring(value, steps):
    return lax.ppermute(value, "mesh", [(p, (p + steps) % PARTS) for p in range(PARTS)])


def from_above(value, sections, steps, cyclic):
    pairs = [
        (s * PARTS + p, (s - 1) % sections * PARTS + (p + steps) % PARTS)
        for s in range(0 if cyclic else 1, sections)
        for p in range(PARTS)
    ]
    return lax.ppermute(value, ("section", "mesh"), pairs)


def split_sum(keep, received):
    half = keep.shape[0] // 2
    return add(keep[:half], received[:half]), add(keep[half:], received[half:])


def per_device(
    saved_inputs, w_query, w_key, w_value, w_out, pending, top_grads, key_blocks, counts, plan
):
    sections = lax.axis_size("section")
    ids = jnp.stack([lax.axis_index("section"), lax.axis_index("mesh")]).astype(jnp.int32)
    weights = (w_query[0], w_key[0], w_value[0])
    wo = w_out[0]
    g0, top = pending[0], top_grads[0]
    info, last0, first0, x0, x1 = prepare(ids, plan, counts, key_blocks, saved_inputs[0])
    x_edges0 = (ring(last0, 1), ring(first0, -1))
    normed, q, k, v, later_last, later_first = project_own((x0, x1), g0, weights)
    later = (ring(later_last, 1), ring(later_first, -1))
    qh, kh, vh = project_edge(x_edges0, weights, "project_edge0")
    att0, dq0, dk, dv, stats_first, stats_last = attend(info, 0, q, k, v, kh, vh, wo, (g0,))
    stats = (ring(stats_last, 1), ring(stats_first, -1))
    gah, part = ahead(later, wo, dq0, weights[0], "ahead0")
    gk0, gv0 = cross(info, 0, qh, gah, k, v, stats, dk, dv)
    gx0, edge_last, edge_first = grad(info, 0, part, gk0, gv0, weights, x0, (g0, top))
    passed = from_above(gx0, sections, 0, False)
    g_edges1 = (
        from_above(edge_last, sections, 1, True),
        from_above(edge_first, sections, -1, True),
    )
    qh, kh, vh = project_edge(later, weights, "project_edge1")
    att1, dq1, dk, dv, stats_first, stats_last, g1 = attend(
        info, 1, q, k, v, kh, vh, wo, (passed, top)
    )
    stats = (ring(stats_last, 1), ring(stats_first, -1))
    g_edges1, att1, dq1 = lax.optimization_barrier((g_edges1, att1, dq1))
    both = (normed, normed)

    def first_exchange(orders, left, offset, right, name):
        parts = weight_part(info, orders, left, offset, right, f"weight_{name}")
        return [
            (order, keep, swap(send, order[0]))
            for order, keep, send in zip(orders, parts[::2], parts[1::2])
        ]

    def halves_of(group):
        return [(order, *split_sum(keep, received)) for order, keep, received in group]

    early = [
        first_exchange(EARLY_ORDERS[0], both, ROWS, (dq0, dq1), "query"),
        first_exchange(EARLY_ORDERS[1], (att0, att1), 0, (g0, g1), "out"),
    ]
    gah, part = ahead(g_edges1, wo, dq1, weights[0], "ahead1")
    gk1, gv1 = cross(info, 1, qh, gah, k, v, stats, dk, dv)
    early, (gk1, gv1) = lax.optimization_barrier(
        ([[e[1:] for e in group] for group in early], (gk1, gv1))
    )
    early = [
        halves_of([(order, *pair) for order, pair in zip(orders, group)])
        for orders, group in zip(EARLY_ORDERS, early)
    ]
    early_got = [[swap(send, order[1]) for order, _, send in group] for group in early]
    late = [
        first_exchange(LATE_ORDERS[0], both, ROWS, (gk0, gk1), "key"),
        first_exchange(LATE_ORDERS[1], both, ROWS, (gv0, gv1), "value"),
    ]
    (gx1,) = grad(info, 1, part, gk1, gv1, weights, x1, (g1,))
    late = [halves_of(group) for group in late]
    late_sent, early_got = lax.optimization_barrier(
        ([[send for _, _, send in group] for group in late], early_got)
    )
    late_got = [
        [swap(send, order[1]) for (order, _, _), send in zip(group, sent)]
        for group, sent in zip(late, late_sent)
    ]
    ends = []
    for name, groups, got in (("early", early, early_got), ("late", late, late_got)):
        for n, (group, received) in enumerate(zip(groups, got)):
            (order, keep_a, _), (_, keep_b, _) = group
            merged = merge(keep_a, received[0], keep_b, received[1], f"merge_{name}{n}")
            ends.append((order, *merged))
    for stage in (2, 3):
        ends = [
            (order, *split_sum(keep, swap(send, order[stage]))) for order, keep, send in ends
        ]
    totals = []
    for pair in (ends[:2], ends[2:]):
        far = swap(jnp.concatenate([send for _, _, send in pair]), ZZ)
        for n, (_, keep, _) in enumerate(pair):
            totals.append(keep[0].astype(F32) + far[n].astype(F32))
    query, out, key, value = totals
    layer_total = jnp.stack([query, key, value, out], axis=1)
    return (layer_total[None], jnp.stack([gx0, gx1])[:, None])


def solution(mesh):
    in_specs = (
        P("section", None, "mesh", None),
        P("section", None, None),
        P("section", None, None),
        P("section", None, None),
        P("section", None, None),
        P("section", "mesh", None),
        P(None, "mesh", None),
        P("mesh", None),
        P(),
        P(),
    )
    out_specs = (P("section", "mesh", None, None), P(None, "section", "mesh", None))
    return jax.shard_map(
        per_device, mesh=mesh, in_specs=in_specs, out_specs=out_specs, check_vma=False
    )
```

```python
import functools
import math

import jax
import jax.numpy as jnp
from jax import lax
from jax.experimental import pallas as pl
from jax.experimental.pallas import tpu as pltpu
from jax.sharding import PartitionSpec as P

HEADS = 8
BLOCK = 128
ROWS = 256
WIDE = 1024
HEAD_DIM = 128
SECTIONS = 8
VMEM_LIMIT = 16 * 1024 * 1024
EPSILON = 1e-06
SCALE = 1.0 / math.sqrt(HEAD_DIM)
PARTS = 32
UNLISTED = 3e38
BF = jnp.bfloat16
F32 = jnp.float32

AX, BX, AY, BY, ZZ = 8, 24, 1, 3, 4
ORDERS = (
    (AX, AY, BX, BY, ZZ),
    (BX, BY, AX, AY, ZZ),
    (AY, AX, BY, BX, ZZ),
    (BY, BX, AY, AX, ZZ),
)
DEPTH = WIDE // PARTS


def right_dot(left, right):
    return lax.dot_general(
        left, right, (((1,), (1,)), ((), ())), preferred_element_type=jnp.float32
    )


def left_dot(left, right):
    return lax.dot_general(
        left, right, (((0,), (0,)), ((), ())), preferred_element_type=jnp.float32
    )


def dot(left, right):
    return jnp.dot(left, right, preferred_element_type=jnp.float32)


def inverse_rms(x):
    return lax.rsqrt(jnp.mean(x * x, axis=-1, keepdims=True) + EPSILON)


def cost(flops, moved):
    return pl.CostEstimate(flops=int(flops), bytes_accessed=int(moved), transcendentals=0)


def shape(rows, columns, dtype=BF):
    return jax.ShapeDtypeStruct((rows, columns), dtype)


def space(value):
    return pltpu.SMEM if value.dtype == jnp.int32 else pltpu.VMEM


def call(kernel, args, out_shape, scratch, estimate, name):
    return pl.pallas_call(
        kernel,
        out_shape=out_shape,
        in_specs=[pl.BlockSpec(memory_space=space(value)) for value in args],
        out_specs=[pl.BlockSpec(memory_space=space(value)) for value in out_shape],
        scratch_shapes=scratch,
        compiler_params=pltpu.CompilerParams(vmem_limit_bytes=VMEM_LIMIT),
        cost_estimate=estimate,
        name=name,
    )(*args)


def prepare_kernel(block_count, ints, saved, info, edge_last, edge_first, x0, x1):
    section, part = ints[0], ints[1]
    plan_at, counts_at, sections = 2, 2 + 2 * SECTIONS, SECTIONS
    blocks_at = counts_at + block_count
    first, last = slice(0, BLOCK), slice(ROWS - BLOCK, ROWS)
    m0, m1 = ints[plan_at + section], ints[plan_at + sections + section]
    edge_last[...] = saved[m0, last]
    edge_first[...] = saved[m0, first]
    x0[...] = saved[m0]
    x1[...] = saved[m1]
    info[0] = part
    info[1] = section
    for b in range(2):
        for e, j in ((0, 1), (2, 0)):
            listed = ints[blocks_at + 2 * b + j]
            found = ints[counts_at + jnp.maximum(listed, 0)]
            info[2 + 3 * b + e] = jnp.where(listed >= 0, found, 0)
        info[3 + 3 * b] = ints[counts_at + part * 2 + b]


def prepare(ids, plan, counts, key_blocks, saved):
    ints = jnp.concatenate([ids, plan.reshape(-1), counts, key_blocks.reshape(-1)])
    return call(
        functools.partial(prepare_kernel, counts.shape[0]),
        (ints, saved),
        [jax.ShapeDtypeStruct((8,), jnp.int32)]
        + [shape(BLOCK, WIDE)] * 2
        + [shape(ROWS, WIDE)] * 2,
        [],
        cost(0, 6 * ROWS * WIDE * 2),
        "prepare",
    )


def normalised(x):
    x = x.astype(F32)
    return (x * inverse_rms(x)).astype(BF)


def project_own_kernel(xa, xb, g, wq, wk, wv, normed_out, q, k, v, later_last, later_first):
    normed = jnp.concatenate([normalised(xa[...]), normalised(xb[...])], axis=0)
    normed_out[...] = normed
    for rows, later in ((slice(ROWS - BLOCK, ROWS), later_last), (slice(0, BLOCK), later_first)):
        later[:BLOCK, :] = g[rows, :]
        later[BLOCK:, :] = xb[rows, :]
    for weight, out in ((wq, q), (wk, k), (wv, v)):
        out[...] = dot(normed, weight[...]).astype(BF)


def project_own(xs, g, weights):
    rows = 2 * ROWS
    return call(
        project_own_kernel,
        (*xs, g, *weights),
        [shape(rows, WIDE)] * 4 + [shape(ROWS, WIDE)] * 2,
        [],
        cost(6 * rows * WIDE * WIDE, 6 * WIDE * WIDE + 10 * rows * WIDE),
        "project_own",
    )


def project_edge_kernel(xa, xb, wq, wk, wv, q, k, v, *normed_out):
    parts = [normalised(ref[ref.shape[0] - BLOCK :, :]) for ref in (xa, xb)]
    normed = jnp.concatenate(parts, axis=0)
    for out in normed_out:
        out[...] = normed
    for weight, out in ((wq, q), (wk, k), (wv, v)):
        out[...] = dot(normed, weight[...]).astype(BF)


def project_edge(xs, weights, keep_normed, name):
    return call(
        project_edge_kernel,
        (*xs, *weights),
        [shape(ROWS, WIDE)] * (3 + keep_normed),
        [],
        cost(6 * ROWS * WIDE * WIDE, 6 * WIDE * WIDE + 10 * ROWS * WIDE),
        name,
    )


def attend_kernel(tick, info, q, k, v, kh, vh, wo, *rest):
    if tick == 0:
        g, att, dq, dk, dv, stats_first, stats_last = rest
        upstream = g[...]
    else:
        g, top, att, dq, dk, dv, stats_first, stats_last, upstream_out, *pairs = rest
        upstream = jnp.where(info[1] == SECTIONS - 1, top[...], g[...])
        upstream_out[...] = upstream
    ga = right_dot(upstream, wo[...]).astype(BF)
    place = lax.broadcasted_iota(jnp.int32, (3 * BLOCK, 1), 0)
    base = tick * ROWS
    valid = []
    listed = []
    for b in range(2):
        limit = [info[2 + 3 * b + e] for e in range(3)]
        inside = place < jnp.minimum(limit[0], BLOCK)
        for e in (1, 2):
            at = place - e * BLOCK
            inside = inside | ((at >= 0) & (at < jnp.minimum(limit[e], BLOCK)))
        valid.append(inside)
        listed.append(limit[2 * b] > 0)
    for head in range(HEADS):
        sl = slice(head * HEAD_DIM, (head + 1) * HEAD_DIM)
        kx = jnp.concatenate([kh[:BLOCK, sl], k[base : base + ROWS, sl], kh[BLOCK:, sl]], axis=0)
        vx = jnp.concatenate([vh[:BLOCK, sl], v[base : base + ROWS, sl], vh[BLOCK:, sl]], axis=0)
        dk_sum = None
        for b in range(2):
            rows = slice(b * BLOCK, (b + 1) * BLOCK)
            qb, gb = q[base + b * BLOCK : base + (b + 1) * BLOCK, sl], ga[rows, sl]
            kb, vb = kx[b * BLOCK : (b + 3) * BLOCK], vx[b * BLOCK : (b + 3) * BLOCK]
            s = jnp.where(valid[b], right_dot(kb, qb) * SCALE, -jnp.inf)
            peak = jnp.max(s, axis=0, keepdims=True)
            raised = jnp.exp(s - peak)
            total = jnp.sum(raised, axis=0, keepdims=True)
            p = raised * (1.0 / total)
            pb = p.astype(BF)
            att[rows, sl] = left_dot(pb, vb).astype(BF)
            gp = right_dot(vb, gb)
            mid = jnp.sum(p * gp, axis=0, keepdims=True)
            ds = (p * (gp - mid) * SCALE).astype(BF)
            dq[rows, sl] = left_dot(ds, kb).astype(BF)
            own = slice(BLOCK, 3 * BLOCK) if b == 0 else slice(0, 2 * BLOCK)
            if tick == 0:
                dk_now, dv_now = dot(ds[own], qb), dot(pb[own], gb)
            else:
                far = slice(0, BLOCK) if b == 0 else slice(2 * BLOCK, 3 * BLOCK)
                dk_all, dv_all = dot(ds, qb), dot(pb, gb)
                pairs[2][rows, sl] = dk_all[far].astype(BF)
                pairs[3][rows, sl] = dv_all[far].astype(BF)
                dk_now, dv_now = dk_all[own], dv_all[own]
            dk_sum, dv_sum = (
                (dk_now, dv_now) if dk_sum is None else (dk_sum + dk_now, dv_sum + dv_now)
            )
            stats = (stats_first, stats_last)[b]
            stats[head : head + 1, :] = jnp.where(listed[b], peak, UNLISTED)
            stats[HEADS + head : HEADS + head + 1, :] = total
            stats[2 * HEADS + head : 2 * HEADS + head + 1, :] = mid
        dk[:, sl] = dk_sum
        dv[:, sl] = dv_sum
        if tick:
            pairs[0][:, sl] = dk_sum.astype(BF)
            pairs[1][:, sl] = dv_sum.astype(BF)


def attend(info, tick, q, k, v, kh, vh, wo, upstream):
    outs = [shape(ROWS, WIDE)] * 2 + [shape(ROWS, WIDE, F32)] * 2
    outs += [shape(3 * HEADS, BLOCK, F32)] * 2 + [shape(ROWS, WIDE)] * (5 * tick)
    return call(
        functools.partial(attend_kernel, tick),
        (info, q, k, v, kh, vh, wo, *upstream),
        outs,
        [],
        cost(8 * 2 * ROWS * WIDE * WIDE, 12 * ROWS * WIDE * 2),
        f"attend{tick}",
    )


def ahead_kernel(g_prev, g_next, wo, dq, wq, gah, part):
    g_far = jnp.concatenate([g_prev[:BLOCK, :], g_next[:BLOCK, :]], axis=0)
    gah[...] = right_dot(g_far, wo[...]).astype(BF)
    part[...] = right_dot(dq[...], wq[...])


def ahead(g_edges, wo, dq, wq, name):
    return call(
        ahead_kernel,
        (*g_edges, wo, dq, wq),
        [shape(ROWS, WIDE), shape(ROWS, WIDE, F32)],
        [],
        cost(4 * ROWS * WIDE * WIDE, 4 * WIDE * WIDE + 8 * ROWS * WIDE),
        name,
    )


def cross_kernel(tick, info, qh, gah, k, v, s_prev, s_next, dk, dv, gk, gv):
    base = tick * ROWS
    place = lax.broadcasted_iota(jnp.int32, (BLOCK, 1), 0)
    for head in range(HEADS):
        sl = slice(head * HEAD_DIM, (head + 1) * HEAD_DIM)
        for b, stats in enumerate((s_prev, s_next)):
            rows = slice(b * BLOCK, (b + 1) * BLOCK)
            mine = slice(base + b * BLOCK, base + (b + 1) * BLOCK)
            peak, total, mid = (
                stats[at * HEADS + head : at * HEADS + head + 1, :] for at in range(3)
            )
            qb, kb, vb, gb = qh[rows, sl], k[mine, sl], v[mine, sl], gah[rows, sl]
            s = right_dot(kb, qb) * SCALE
            inside = place < info[3 + 3 * b]
            p = jnp.where(inside, jnp.exp(s - peak), 0.0) * (1.0 / total)
            ds = (p * (right_dot(vb, gb) - mid) * SCALE).astype(BF)
            dk_far = dot(ds, qb).astype(BF).astype(F32)
            dv_far = dot(p.astype(BF), gb).astype(BF).astype(F32)
            gk[rows, sl] = (dk[rows, sl] + dk_far).astype(BF)
            gv[rows, sl] = (dv[rows, sl] + dv_far).astype(BF)


def cross(info, tick, qh, gah, k, v, stats, dk, dv):
    return call(
        functools.partial(cross_kernel, tick),
        (info, qh, gah, k, v, *stats, dk, dv),
        [shape(ROWS, WIDE)] * 2,
        [],
        cost(2 * ROWS * WIDE * WIDE, 20 * ROWS * WIDE),
        f"cross{tick}",
    )


def grad_kernel(tick, info, part, gk, gv, wk, wv, x, g, *rest):
    gx = rest[0] if tick else rest[1]
    grad = part[...] + right_dot(gk[...], wk[...]) + right_dot(gv[...], wv[...])
    xf = x[...].astype(F32)
    r = inverse_rms(xf)
    xr = xf * r
    grad_in = r * (grad - xr * jnp.mean(grad * xr, axis=-1, keepdims=True))
    out = (g[...].astype(F32) + grad_in).astype(BF)
    gx[...] = out
    if tick == 0:
        top, _, edge_last, edge_first = rest
        at_bottom = info[1] == 0
        edge_last[...] = jnp.where(at_bottom, top[BLOCK:, :], out[BLOCK:, :])
        edge_first[...] = jnp.where(at_bottom, top[:BLOCK, :], out[:BLOCK, :])


def grad(info, tick, part, gk, gv, weights, x, gs):
    edges = [shape(BLOCK, WIDE)] * (2 - 2 * tick)
    return call(
        functools.partial(grad_kernel, tick),
        (info, part, gk, gv, *weights[1:], x, *gs),
        [shape(ROWS, WIDE)] + edges,
        [],
        cost(4 * ROWS * WIDE * WIDE, 4 * WIDE * WIDE + 12 * ROWS * WIDE),
        f"grad{tick}",
    )


def position(order, q):
    found = 0
    for bit, mask in enumerate(order):
        if (q >> (len(order) - 1 - bit)) & 1:
            found ^= mask
    return found


def weight_kernel(order, offsets, info, *refs):
    count = len(offsets)
    lefts, rights, (keep, send, chunks) = refs[:count], refs[count : 2 * count], refs[2 * count :]
    product = sum(
        left_dot(left[offset : offset + ROWS, :], right[...])
        for left, offset, right in zip(lefts, offsets, rights)
    )
    chunks[...] = product.astype(BF).reshape(chunks.shape)
    me = info[0]
    half = PARTS // 2
    for q in range(PARTS):
        out = keep if q < half else send
        out[q % half] = chunks[lax.bitwise_xor(jnp.int32(position(order, q)), me)]


def weight_part(info, order, lefts, offsets, rights, name):
    half = jax.ShapeDtypeStruct((PARTS // 2, DEPTH, WIDE), BF)
    return call(
        functools.partial(weight_kernel, order, offsets),
        (info, *lefts, *rights),
        [half] * 2,
        [pltpu.VMEM((PARTS, DEPTH, WIDE), BF)],
        cost(4 * ROWS * WIDE * WIDE, 8 * ROWS * WIDE + 2 * WIDE * WIDE),
        name,
    )


def swap(value, mask):
    return lax.ppermute(value, "mesh", [(p, p ^ mask) for p in range(PARTS)])


def add(left, right):
    return (left.astype(F32) + right.astype(F32)).astype(BF)


def ring(value, steps):
    return lax.ppermute(value, "mesh", [(p, (p + steps) % PARTS) for p in range(PARTS)])


def from_above(value, sections, steps, cyclic):
    pairs = [
        (s * PARTS + p, (s - 1) % sections * PARTS + (p + steps) % PARTS)
        for s in range(0 if cyclic else 1, sections)
        for p in range(PARTS)
    ]
    return lax.ppermute(value, ("section", "mesh"), pairs)


def split_sum(keep, received):
    half = keep.shape[0] // 2
    return add(keep[:half], received[:half]), add(keep[half:], received[half:])


def per_device(
    saved_inputs, w_query, w_key, w_value, w_out, pending, top_grads, key_blocks, counts, plan
):
    sections = lax.axis_size("section")
    ids = jnp.stack([lax.axis_index("section"), lax.axis_index("mesh")]).astype(jnp.int32)
    weights = (w_query[0], w_key[0], w_value[0])
    wo = w_out[0]
    g0, top = pending[0], top_grads[0]
    info, last0, first0, x0, x1 = prepare(ids, plan, counts, key_blocks, saved_inputs[0])
    x_edges0 = (ring(last0, 1), ring(first0, -1))
    normed, q, k, v, later_last, later_first = project_own((x0, x1), g0, weights)
    later = (ring(later_last, 1), ring(later_first, -1))
    qh, kh, vh = project_edge(x_edges0, weights, False, "project_edge0")
    att0, dq0, dk, dv, stats_first, stats_last = attend(info, 0, q, k, v, kh, vh, wo, (g0,))
    stats = (ring(stats_last, 1), ring(stats_first, -1))
    gah, part = ahead(later, wo, dq0, weights[0], "ahead0")
    gk0, gv0 = cross(info, 0, qh, gah, k, v, stats, dk, dv)
    gx0, edge_last, edge_first = grad(info, 0, part, gk0, gv0, weights, x0, (g0, top))
    passed = from_above(gx0, sections, 0, False)
    qh, kh, vh, normed_far = project_edge(later, weights, True, "project_edge1")
    att1, dq1, dk, dv, stats_first, stats_last, g1, dk_own, dv_own, dk_far, dv_far = attend(
        info, 1, q, k, v, kh, vh, wo, (passed, top)
    )
    lefts = (normed, normed, normed_far)
    sums = []
    for w, left, offsets, right in (
        (3, (att0, att1), (0, 0), (g0, g1)),
        (0, (normed, normed), (0, ROWS), (dq0, dq1)),
        (1, lefts, (0, ROWS, 0), (gk0, dk_own, dk_far)),
        (2, lefts, (0, ROWS, 0), (gv0, dv_own, dv_far)),
    ):
        keep, send = weight_part(info, ORDERS[w], left, offsets, right, f"weight{w}")
        sums.append((w, keep, swap(send, ORDERS[w][0])))
    kept, sent_on = lax.optimization_barrier(
        ([keep for _, keep, _ in sums], (edge_last, edge_first, stats_first, stats_last))
    )
    sums = [(w, keep, received) for (w, _, received), keep in zip(sums, kept)]
    edge_last, edge_first, stats_first, stats_last = sent_on
    g_edges1 = (
        from_above(edge_last, sections, 1, True),
        from_above(edge_first, sections, -1, True),
    )
    stats = (ring(stats_last, 1), ring(stats_first, -1))
    (g_edges1, stats), received = lax.optimization_barrier(
        ((g_edges1, stats), [received for _, _, received in sums])
    )
    sums = [(w, keep, got) for (w, keep, _), got in zip(sums, received)]
    gah, part = ahead(g_edges1, wo, dq1, weights[0], "ahead1")
    gk1, gv1 = cross(info, 1, qh, gah, k, v, stats, dk, dv)
    (gx1,) = grad(info, 1, part, gk1, gv1, weights, x1, (g1,))
    for stage in (1, 2, 3):
        pairs = [(w, *split_sum(keep, received)) for w, keep, received in sums]
        if stage == 2:
            gx1, sends = lax.optimization_barrier((gx1, [send for _, _, send in pairs]))
            pairs = [(w, keep, send) for (w, keep, _), send in zip(pairs, sends)]
        sums = [(w, keep, swap(send, ORDERS[w][stage])) for w, keep, send in pairs]
    totals = {}
    for group in (sums[:2], sums[2:]):
        pairs = [(w, *split_sum(keep, received)) for w, keep, received in group]
        far = swap(jnp.concatenate([send for _, _, send in pairs]), ZZ)
        for n, (w, keep, _) in enumerate(pairs):
            totals[w] = keep[0].astype(F32) + far[n].astype(F32)
    layer_total = jnp.stack([totals[w] for w in range(4)], axis=1)
    return (layer_total[None], jnp.stack([gx0, gx1])[:, None])


def solution(mesh):
    in_specs = (
        P("section", None, "mesh", None),
        P("section", None, None),
        P("section", None, None),
        P("section", None, None),
        P("section", None, None),
        P("section", "mesh", None),
        P(None, "mesh", None),
        P("mesh", None),
        P(),
        P(),
    )
    out_specs = (P("section", "mesh", None, None), P(None, "section", "mesh", None))
    return jax.shard_map(
        per_device, mesh=mesh, in_specs=in_specs, out_specs=out_specs, check_vma=False
    )
```

```python
import functools
import math

import jax
import jax.numpy as jnp
from jax import lax
from jax.experimental import pallas as pl
from jax.experimental.pallas import tpu as pltpu
from jax.sharding import PartitionSpec as P

HEADS = 8
BLOCK = 128
ROWS = 256
WIDE = 1024
HEAD_DIM = 128
SECTIONS = 8
VMEM_LIMIT = 16 * 1024 * 1024
EPSILON = 1e-06
SCALE = 1.0 / math.sqrt(HEAD_DIM)
PARTS = 32
UNLISTED = 3e38
EDGES_BEFORE = (3,)
GRAD_BEFORE = 3
BF = jnp.bfloat16
F32 = jnp.float32

AX, BX, AY, BY, ZZ = 8, 24, 1, 3, 4
ORDERS = (
    (AX, AY, BX, BY, ZZ),
    (BX, BY, AX, AY, ZZ),
    (AY, AX, BY, BX, ZZ),
    (BY, BX, AY, AX, ZZ),
)
DEPTH = WIDE // PARTS


def right_dot(left, right):
    return lax.dot_general(
        left, right, (((1,), (1,)), ((), ())), preferred_element_type=jnp.float32
    )


def left_dot(left, right):
    return lax.dot_general(
        left, right, (((0,), (0,)), ((), ())), preferred_element_type=jnp.float32
    )


def dot(left, right):
    return jnp.dot(left, right, preferred_element_type=jnp.float32)


def inverse_rms(x):
    return lax.rsqrt(jnp.mean(x * x, axis=-1, keepdims=True) + EPSILON)


def cost(flops, moved):
    return pl.CostEstimate(flops=int(flops), bytes_accessed=int(moved), transcendentals=0)


def shape(rows, columns, dtype=BF):
    return jax.ShapeDtypeStruct((rows, columns), dtype)


def space(value):
    return pltpu.SMEM if value.dtype == jnp.int32 else pltpu.VMEM


def call(kernel, args, out_shape, scratch, estimate, name):
    return pl.pallas_call(
        kernel,
        out_shape=out_shape,
        in_specs=[pl.BlockSpec(memory_space=space(value)) for value in args],
        out_specs=[pl.BlockSpec(memory_space=space(value)) for value in out_shape],
        scratch_shapes=scratch,
        compiler_params=pltpu.CompilerParams(vmem_limit_bytes=VMEM_LIMIT),
        cost_estimate=estimate,
        name=name,
    )(*args)


def prepare_kernel(block_count, ints, saved, info, edge_last, edge_first, x0, x1):
    section, part = ints[0], ints[1]
    plan_at, counts_at, sections = 2, 2 + 2 * SECTIONS, SECTIONS
    blocks_at = counts_at + block_count
    first, last = slice(0, BLOCK), slice(ROWS - BLOCK, ROWS)
    m0, m1 = ints[plan_at + section], ints[plan_at + sections + section]
    edge_last[...] = saved[m0, last]
    edge_first[...] = saved[m0, first]
    x0[...] = saved[m0]
    x1[...] = saved[m1]
    info[0] = part
    info[1] = section
    for b in range(2):
        for e, j in ((0, 1), (2, 0)):
            listed = ints[blocks_at + 2 * b + j]
            found = ints[counts_at + jnp.maximum(listed, 0)]
            info[2 + 3 * b + e] = jnp.where(listed >= 0, found, 0)
        info[3 + 3 * b] = ints[counts_at + part * 2 + b]


def prepare(ids, plan, counts, key_blocks, saved):
    ints = jnp.concatenate([ids, plan.reshape(-1), counts, key_blocks.reshape(-1)])
    return call(
        functools.partial(prepare_kernel, counts.shape[0]),
        (ints, saved),
        [jax.ShapeDtypeStruct((8,), jnp.int32)]
        + [shape(BLOCK, WIDE)] * 2
        + [shape(ROWS, WIDE)] * 2,
        [],
        cost(0, 6 * ROWS * WIDE * 2),
        "prepare",
    )


def normalised(x):
    x = x.astype(F32)
    return (x * inverse_rms(x)).astype(BF)


def project_own_kernel(xa, xb, g, wq, wk, wv, normed_out, q, k, v, later_last, later_first):
    normed = jnp.concatenate([normalised(xa[...]), normalised(xb[...])], axis=0)
    normed_out[...] = normed
    for rows, later in ((slice(ROWS - BLOCK, ROWS), later_last), (slice(0, BLOCK), later_first)):
        later[:BLOCK, :] = g[rows, :]
        later[BLOCK:, :] = xb[rows, :]
    for weight, out in ((wq, q), (wk, k), (wv, v)):
        out[...] = dot(normed, weight[...]).astype(BF)


def project_own(xs, g, weights):
    rows = 2 * ROWS
    return call(
        project_own_kernel,
        (*xs, g, *weights),
        [shape(rows, WIDE)] * 4 + [shape(ROWS, WIDE)] * 2,
        [],
        cost(6 * rows * WIDE * WIDE, 6 * WIDE * WIDE + 10 * rows * WIDE),
        "project_own",
    )


def project_edge_kernel(xa, xb, wq, wk, wv, q, k, v, *normed_out):
    parts = [normalised(ref[ref.shape[0] - BLOCK :, :]) for ref in (xa, xb)]
    normed = jnp.concatenate(parts, axis=0)
    for out in normed_out:
        out[...] = normed
    for weight, out in ((wq, q), (wk, k), (wv, v)):
        out[...] = dot(normed, weight[...]).astype(BF)


def project_edge(xs, weights, keep_normed, name):
    return call(
        project_edge_kernel,
        (*xs, *weights),
        [shape(ROWS, WIDE)] * (3 + keep_normed),
        [],
        cost(6 * ROWS * WIDE * WIDE, 6 * WIDE * WIDE + 10 * ROWS * WIDE),
        name,
    )


def attend_kernel(tick, info, q, k, v, kh, vh, wo, *rest):
    if tick == 0:
        g, att, dq, dk, dv, stats_first, stats_last = rest
        upstream = g[...]
    else:
        g, top, att, dq, dk, dv, stats_first, stats_last, upstream_out, *pairs = rest
        upstream = jnp.where(info[1] == SECTIONS - 1, top[...], g[...])
        upstream_out[...] = upstream
    ga = right_dot(upstream, wo[...]).astype(BF)
    place = lax.broadcasted_iota(jnp.int32, (3 * BLOCK, 1), 0)
    base = tick * ROWS
    valid = []
    listed = []
    for b in range(2):
        limit = [info[2 + 3 * b + e] for e in range(3)]
        inside = place < jnp.minimum(limit[0], BLOCK)
        for e in (1, 2):
            at = place - e * BLOCK
            inside = inside | ((at >= 0) & (at < jnp.minimum(limit[e], BLOCK)))
        valid.append(inside)
        listed.append(limit[2 * b] > 0)
    for head in range(HEADS):
        sl = slice(head * HEAD_DIM, (head + 1) * HEAD_DIM)
        kx = jnp.concatenate([kh[:BLOCK, sl], k[base : base + ROWS, sl], kh[BLOCK:, sl]], axis=0)
        vx = jnp.concatenate([vh[:BLOCK, sl], v[base : base + ROWS, sl], vh[BLOCK:, sl]], axis=0)
        dk_sum = None
        for b in range(2):
            rows = slice(b * BLOCK, (b + 1) * BLOCK)
            qb, gb = q[base + b * BLOCK : base + (b + 1) * BLOCK, sl], ga[rows, sl]
            kb, vb = kx[b * BLOCK : (b + 3) * BLOCK], vx[b * BLOCK : (b + 3) * BLOCK]
            s = jnp.where(valid[b], right_dot(kb, qb) * SCALE, -jnp.inf)
            peak = jnp.max(s, axis=0, keepdims=True)
            raised = jnp.exp(s - peak)
            total = jnp.sum(raised, axis=0, keepdims=True)
            p = raised * (1.0 / total)
            pb = p.astype(BF)
            att[rows, sl] = left_dot(pb, vb).astype(BF)
            gp = right_dot(vb, gb)
            mid = jnp.sum(p * gp, axis=0, keepdims=True)
            ds = (p * (gp - mid) * SCALE).astype(BF)
            dq[rows, sl] = left_dot(ds, kb).astype(BF)
            own = slice(BLOCK, 3 * BLOCK) if b == 0 else slice(0, 2 * BLOCK)
            if tick == 0:
                dk_now, dv_now = dot(ds[own], qb), dot(pb[own], gb)
            else:
                far = slice(0, BLOCK) if b == 0 else slice(2 * BLOCK, 3 * BLOCK)
                dk_all, dv_all = dot(ds, qb), dot(pb, gb)
                pairs[2][rows, sl] = dk_all[far].astype(BF)
                pairs[3][rows, sl] = dv_all[far].astype(BF)
                dk_now, dv_now = dk_all[own], dv_all[own]
            dk_sum, dv_sum = (
                (dk_now, dv_now) if dk_sum is None else (dk_sum + dk_now, dv_sum + dv_now)
            )
            stats = (stats_first, stats_last)[b]
            stats[head : head + 1, :] = jnp.where(listed[b], peak, UNLISTED)
            stats[HEADS + head : HEADS + head + 1, :] = total
            stats[2 * HEADS + head : 2 * HEADS + head + 1, :] = mid
        dk[:, sl] = dk_sum
        dv[:, sl] = dv_sum
        if tick:
            pairs[0][:, sl] = dk_sum.astype(BF)
            pairs[1][:, sl] = dv_sum.astype(BF)


def attend(info, tick, q, k, v, kh, vh, wo, upstream):
    outs = [shape(ROWS, WIDE)] * 2 + [shape(ROWS, WIDE, F32)] * 2
    outs += [shape(3 * HEADS, BLOCK, F32)] * 2 + [shape(ROWS, WIDE)] * (5 * tick)
    return call(
        functools.partial(attend_kernel, tick),
        (info, q, k, v, kh, vh, wo, *upstream),
        outs,
        [],
        cost(8 * 2 * ROWS * WIDE * WIDE, 12 * ROWS * WIDE * 2),
        f"attend{tick}",
    )


def ahead_kernel(g_prev, g_next, wo, dq, wq, gah, part):
    g_far = jnp.concatenate([g_prev[:BLOCK, :], g_next[:BLOCK, :]], axis=0)
    gah[...] = right_dot(g_far, wo[...]).astype(BF)
    part[...] = right_dot(dq[...], wq[...])


def ahead(g_edges, wo, dq, wq, name):
    return call(
        ahead_kernel,
        (*g_edges, wo, dq, wq),
        [shape(ROWS, WIDE), shape(ROWS, WIDE, F32)],
        [],
        cost(4 * ROWS * WIDE * WIDE, 4 * WIDE * WIDE + 8 * ROWS * WIDE),
        name,
    )


def cross_kernel(tick, info, qh, gah, k, v, s_prev, s_next, dk, dv, gk, gv):
    base = tick * ROWS
    place = lax.broadcasted_iota(jnp.int32, (BLOCK, 1), 0)
    for head in range(HEADS):
        sl = slice(head * HEAD_DIM, (head + 1) * HEAD_DIM)
        for b, stats in enumerate((s_prev, s_next)):
            rows = slice(b * BLOCK, (b + 1) * BLOCK)
            mine = slice(base + b * BLOCK, base + (b + 1) * BLOCK)
            peak, total, mid = (
                stats[at * HEADS + head : at * HEADS + head + 1, :] for at in range(3)
            )
            qb, kb, vb, gb = qh[rows, sl], k[mine, sl], v[mine, sl], gah[rows, sl]
            s = right_dot(kb, qb) * SCALE
            inside = place < info[3 + 3 * b]
            p = jnp.where(inside, jnp.exp(s - peak), 0.0) * (1.0 / total)
            ds = (p * (right_dot(vb, gb) - mid) * SCALE).astype(BF)
            dk_far = dot(ds, qb).astype(BF).astype(F32)
            dv_far = dot(p.astype(BF), gb).astype(BF).astype(F32)
            gk[rows, sl] = (dk[rows, sl] + dk_far).astype(BF)
            gv[rows, sl] = (dv[rows, sl] + dv_far).astype(BF)


def cross(info, tick, qh, gah, k, v, stats, dk, dv):
    return call(
        functools.partial(cross_kernel, tick),
        (info, qh, gah, k, v, *stats, dk, dv),
        [shape(ROWS, WIDE)] * 2,
        [],
        cost(2 * ROWS * WIDE * WIDE, 20 * ROWS * WIDE),
        f"cross{tick}",
    )


def grad_kernel(tick, info, part, gk, gv, wk, wv, x, g, *rest):
    grad = part[...] + right_dot(gk[...], wk[...]) + right_dot(gv[...], wv[...])
    xf = x[...].astype(F32)
    r = inverse_rms(xf)
    xr = xf * r
    grad_in = r * (grad - xr * jnp.mean(grad * xr, axis=-1, keepdims=True))
    out = (g[...].astype(F32) + grad_in).astype(BF)
    if tick:
        earlier, gx = rest
        gx[0] = earlier[...]
        gx[1] = out
    else:
        top, gx, edge_last, edge_first = rest
        gx[...] = out
        at_bottom = info[1] == 0
        edge_last[...] = jnp.where(at_bottom, top[BLOCK:, :], out[BLOCK:, :])
        edge_first[...] = jnp.where(at_bottom, top[:BLOCK, :], out[:BLOCK, :])


def grad(info, tick, part, gk, gv, weights, x, gs):
    both = [jax.ShapeDtypeStruct((2, ROWS, WIDE), BF)]
    return call(
        functools.partial(grad_kernel, tick),
        (info, part, gk, gv, *weights[1:], x, *gs),
        both if tick else [shape(ROWS, WIDE)] + [shape(BLOCK, WIDE)] * 2,
        [],
        cost(4 * ROWS * WIDE * WIDE, 4 * WIDE * WIDE + 12 * ROWS * WIDE),
        f"grad{tick}",
    )


def position(order, q):
    found = 0
    for bit, mask in enumerate(order):
        if (q >> (len(order) - 1 - bit)) & 1:
            found ^= mask
    return found


def weight_kernel(order, offsets, info, *refs):
    count = len(offsets)
    lefts, rights, (keep, send, chunks) = refs[:count], refs[count : 2 * count], refs[2 * count :]
    product = sum(
        left_dot(left[offset : offset + ROWS, :], right[...])
        for left, offset, right in zip(lefts, offsets, rights)
    )
    chunks[...] = product.astype(BF).reshape(chunks.shape)
    me = info[0]
    half = PARTS // 2
    for q in range(PARTS):
        out = keep if q < half else send
        out[q % half] = chunks[lax.bitwise_xor(jnp.int32(position(order, q)), me)]


def weight_part(info, order, lefts, offsets, rights, name):
    half = jax.ShapeDtypeStruct((PARTS // 2, DEPTH, WIDE), BF)
    return call(
        functools.partial(weight_kernel, order, offsets),
        (info, *lefts, *rights),
        [half] * 2,
        [pltpu.VMEM((PARTS, DEPTH, WIDE), BF)],
        cost(4 * ROWS * WIDE * WIDE, 8 * ROWS * WIDE + 2 * WIDE * WIDE),
        name,
    )


def swap(value, mask):
    return lax.ppermute(value, "mesh", [(p, p ^ mask) for p in range(PARTS)])


def add(left, right):
    return (left.astype(F32) + right.astype(F32)).astype(BF)


def ring(value, steps):
    return lax.ppermute(value, "mesh", [(p, (p + steps) % PARTS) for p in range(PARTS)])


def from_above(value, sections, steps, cyclic):
    pairs = [
        (s * PARTS + p, (s - 1) % sections * PARTS + (p + steps) % PARTS)
        for s in range(0 if cyclic else 1, sections)
        for p in range(PARTS)
    ]
    return lax.ppermute(value, ("section", "mesh"), pairs)


def split_sum(keep, received):
    half = keep.shape[0] // 2
    return add(keep[:half], received[:half]), add(keep[half:], received[half:])


def per_device(
    saved_inputs, w_query, w_key, w_value, w_out, pending, top_grads, key_blocks, counts, plan
):
    sections = lax.axis_size("section")
    ids = jnp.stack([lax.axis_index("section"), lax.axis_index("mesh")]).astype(jnp.int32)
    weights = (w_query[0], w_key[0], w_value[0])
    wo = w_out[0]
    g0, top = pending[0], top_grads[0]
    info, last0, first0, x0, x1 = prepare(ids, plan, counts, key_blocks, saved_inputs[0])
    x_edges0 = (ring(last0, 1), ring(first0, -1))
    normed, q, k, v, later_last, later_first = project_own((x0, x1), g0, weights)
    later = (ring(later_last, 1), ring(later_first, -1))
    qh, kh, vh = project_edge(x_edges0, weights, False, "project_edge0")
    att0, dq0, dk, dv, stats_first, stats_last = attend(info, 0, q, k, v, kh, vh, wo, (g0,))
    stats = (ring(stats_last, 1), ring(stats_first, -1))
    gah, part = ahead(later, wo, dq0, weights[0], "ahead0")
    gk0, gv0 = cross(info, 0, qh, gah, k, v, stats, dk, dv)
    gx0, edge_last, edge_first = grad(info, 0, part, gk0, gv0, weights, x0, (g0, top))
    passed = from_above(gx0, sections, 0, False)
    qh, kh, vh, normed_far = project_edge(later, weights, True, "project_edge1")
    passed, edge_last, edge_first = lax.optimization_barrier((passed, edge_last, edge_first))
    g_edges1 = (
        from_above(edge_last, sections, 1, True),
        from_above(edge_first, sections, -1, True),
    )
    att1, dq1, dk, dv, stats_first, stats_last, g1, dk_own, dv_own, dk_far, dv_far = attend(
        info, 1, q, k, v, kh, vh, wo, (passed, top)
    )
    lefts = (normed, normed, normed_far)
    sums = []
    for w, left, offsets, right in (
        (1, lefts, (0, ROWS, 0), (gk0, dk_own, dk_far)),
        (2, lefts, (0, ROWS, 0), (gv0, dv_own, dv_far)),
        (0, (normed, normed), (0, ROWS), (dq0, dq1)),
        (3, (att0, att1), (0, 0), (g0, g1)),
    ):
        if w in EDGES_BEFORE:
            g_edges1, right = lax.optimization_barrier((g_edges1, right))
        keep, send = weight_part(info, ORDERS[w], left, offsets, right, f"weight{w}")
        sums.append((w, keep, swap(send, ORDERS[w][0])))
    (stats_first, stats_last), received = lax.optimization_barrier(
        ((stats_first, stats_last), [received for _, _, received in sums])
    )
    sums = [(w, keep, got) for (w, keep, _), got in zip(sums, received)]
    stats = (ring(stats_last, 1), ring(stats_first, -1))
    gah, part = ahead(g_edges1, wo, dq1, weights[0], "ahead1")
    gk1, gv1 = cross(info, 1, qh, gah, k, v, stats, dk, dv)
    (gx,) = grad(info, 1, part, gk1, gv1, weights, x1, (g1, gx0))
    for stage in (1, 2, 3):
        pairs = [(w, *split_sum(keep, received)) for w, keep, received in sums]
        if stage == GRAD_BEFORE:
            gx, sends = lax.optimization_barrier((gx, [send for _, _, send in pairs]))
            pairs = [(w, keep, send) for (w, keep, _), send in zip(pairs, sends)]
        sums = [(w, keep, swap(send, ORDERS[w][stage])) for w, keep, send in pairs]
    totals = {}
    for group in (sums[:2], sums[2:]):
        pairs = [(w, *split_sum(keep, received)) for w, keep, received in group]
        far = swap(jnp.concatenate([send for _, _, send in pairs]), ZZ)
        for n, (w, keep, _) in enumerate(pairs):
            totals[w] = keep[0].astype(F32) + far[n].astype(F32)
    layer_total = jnp.stack([totals[w] for w in range(4)], axis=1)
    return (layer_total[None], gx[:, None])


def solution(mesh):
    in_specs = (
        P("section", None, "mesh", None),
        P("section", None, None),
        P("section", None, None),
        P("section", None, None),
        P("section", None, None),
        P("section", "mesh", None),
        P(None, "mesh", None),
        P("mesh", None),
        P(),
        P(),
    )
    out_specs = (P("section", "mesh", None, None), P(None, "section", "mesh", None))
    return jax.shard_map(
        per_device, mesh=mesh, in_specs=in_specs, out_specs=out_specs, check_vma=False
    )
```

```python
import functools
import math

import jax
import jax.numpy as jnp
from jax import lax
from jax.experimental import pallas as pl
from jax.experimental.pallas import tpu as pltpu
from jax.sharding import PartitionSpec as P

HEADS = 8
BLOCK = 128
ROWS = 256
WIDE = 1024
HEAD_DIM = 128
SECTIONS = 8
VMEM_LIMIT = 16 * 1024 * 1024
EPSILON = 1e-06
SCALE = 1.0 / math.sqrt(HEAD_DIM)
PARTS = 32
UNLISTED = 3e38
GRAD_BEFORE = 3
BF = jnp.bfloat16
F32 = jnp.float32

AX, BX, AY, BY, ZZ = 8, 24, 1, 3, 4
ORDERS = (
    (AX, AY, BX, BY, ZZ),
    (BX, BY, AX, AY, ZZ),
    (AY, AX, BY, BX, ZZ),
    (BY, BX, AY, AX, ZZ),
)
DEPTH = WIDE // PARTS


def right_dot(left, right):
    return lax.dot_general(
        left, right, (((1,), (1,)), ((), ())), preferred_element_type=jnp.float32
    )


def left_dot(left, right):
    return lax.dot_general(
        left, right, (((0,), (0,)), ((), ())), preferred_element_type=jnp.float32
    )


def dot(left, right):
    return jnp.dot(left, right, preferred_element_type=jnp.float32)


def inverse_rms(x):
    return lax.rsqrt(jnp.mean(x * x, axis=-1, keepdims=True) + EPSILON)


def cost(flops, moved):
    return pl.CostEstimate(flops=int(flops), bytes_accessed=int(moved), transcendentals=0)


def shape(rows, columns, dtype=BF):
    return jax.ShapeDtypeStruct((rows, columns), dtype)


def space(value):
    return pltpu.SMEM if value.dtype == jnp.int32 else pltpu.VMEM


def call(kernel, args, out_shape, scratch, estimate, name):
    return pl.pallas_call(
        kernel,
        out_shape=out_shape,
        in_specs=[pl.BlockSpec(memory_space=space(value)) for value in args],
        out_specs=[pl.BlockSpec(memory_space=space(value)) for value in out_shape],
        scratch_shapes=scratch,
        compiler_params=pltpu.CompilerParams(vmem_limit_bytes=VMEM_LIMIT),
        cost_estimate=estimate,
        name=name,
    )(*args)


def prepare_kernel(block_count, ints, saved, info, edge_last, edge_first, x0, x1):
    section, part = ints[0], ints[1]
    plan_at, counts_at, sections = 2, 2 + 2 * SECTIONS, SECTIONS
    blocks_at = counts_at + block_count
    first, last = slice(0, BLOCK), slice(ROWS - BLOCK, ROWS)
    m0, m1 = ints[plan_at + section], ints[plan_at + sections + section]
    edge_last[...] = saved[m0, last]
    edge_first[...] = saved[m0, first]
    x0[...] = saved[m0]
    x1[...] = saved[m1]
    info[0] = part
    info[1] = section
    for b in range(2):
        for e, j in ((0, 1), (2, 0)):
            listed = ints[blocks_at + 2 * b + j]
            found = ints[counts_at + jnp.maximum(listed, 0)]
            info[2 + 3 * b + e] = jnp.where(listed >= 0, found, 0)
        info[3 + 3 * b] = ints[counts_at + part * 2 + b]


def prepare(ids, plan, counts, key_blocks, saved):
    ints = jnp.concatenate([ids, plan.reshape(-1), counts, key_blocks.reshape(-1)])
    return call(
        functools.partial(prepare_kernel, counts.shape[0]),
        (ints, saved),
        [jax.ShapeDtypeStruct((8,), jnp.int32)]
        + [shape(BLOCK, WIDE)] * 2
        + [shape(ROWS, WIDE)] * 2,
        [],
        cost(0, 6 * ROWS * WIDE * 2),
        "prepare",
    )


def normalised(x):
    x = x.astype(F32)
    return (x * inverse_rms(x)).astype(BF)


def project_own_kernel(xa, xb, g, wq, wk, wv, normed_out, q, k, v, later_last, later_first):
    normed = jnp.concatenate([normalised(xa[...]), normalised(xb[...])], axis=0)
    normed_out[...] = normed
    for rows, later in ((slice(ROWS - BLOCK, ROWS), later_last), (slice(0, BLOCK), later_first)):
        later[:BLOCK, :] = g[rows, :]
        later[BLOCK:, :] = xb[rows, :]
    for weight, out in ((wq, q), (wk, k), (wv, v)):
        out[...] = dot(normed, weight[...]).astype(BF)


def project_own(xs, g, weights):
    rows = 2 * ROWS
    return call(
        project_own_kernel,
        (*xs, g, *weights),
        [shape(rows, WIDE)] * 4 + [shape(ROWS, WIDE)] * 2,
        [],
        cost(6 * rows * WIDE * WIDE, 6 * WIDE * WIDE + 10 * rows * WIDE),
        "project_own",
    )


def project_edge_kernel(xa, xb, wq, wk, wv, q, k, v, *normed_out):
    parts = [normalised(ref[ref.shape[0] - BLOCK :, :]) for ref in (xa, xb)]
    normed = jnp.concatenate(parts, axis=0)
    for out in normed_out:
        out[...] = normed
    for weight, out in ((wq, q), (wk, k), (wv, v)):
        out[...] = dot(normed, weight[...]).astype(BF)


def project_edge(xs, weights, keep_normed, name):
    return call(
        project_edge_kernel,
        (*xs, *weights),
        [shape(ROWS, WIDE)] * (3 + keep_normed),
        [],
        cost(6 * ROWS * WIDE * WIDE, 6 * WIDE * WIDE + 10 * ROWS * WIDE),
        name,
    )


def attend_kernel(tick, info, q, k, v, kh, vh, wo, *rest):
    if tick == 0:
        g, att, dq, dk, dv, stats_first, stats_last = rest
        upstream = g[...]
    else:
        g, top, att, dq, dk, dv, stats_first, stats_last, upstream_out, *pairs = rest
        upstream = jnp.where(info[1] == SECTIONS - 1, top[...], g[...])
        upstream_out[...] = upstream
    ga = right_dot(upstream, wo[...]).astype(BF)
    place = lax.broadcasted_iota(jnp.int32, (3 * BLOCK, 1), 0)
    base = tick * ROWS
    valid = []
    listed = []
    for b in range(2):
        limit = [info[2 + 3 * b + e] for e in range(3)]
        inside = place < jnp.minimum(limit[0], BLOCK)
        for e in (1, 2):
            at = place - e * BLOCK
            inside = inside | ((at >= 0) & (at < jnp.minimum(limit[e], BLOCK)))
        valid.append(inside)
        listed.append(limit[2 * b] > 0)
    for head in range(HEADS):
        sl = slice(head * HEAD_DIM, (head + 1) * HEAD_DIM)
        kx = jnp.concatenate([kh[:BLOCK, sl], k[base : base + ROWS, sl], kh[BLOCK:, sl]], axis=0)
        vx = jnp.concatenate([vh[:BLOCK, sl], v[base : base + ROWS, sl], vh[BLOCK:, sl]], axis=0)
        dk_sum = None
        for b in range(2):
            rows = slice(b * BLOCK, (b + 1) * BLOCK)
            qb, gb = q[base + b * BLOCK : base + (b + 1) * BLOCK, sl], ga[rows, sl]
            kb, vb = kx[b * BLOCK : (b + 3) * BLOCK], vx[b * BLOCK : (b + 3) * BLOCK]
            s = jnp.where(valid[b], right_dot(kb, qb) * SCALE, -jnp.inf)
            peak = jnp.max(s, axis=0, keepdims=True)
            raised = jnp.exp(s - peak)
            total = jnp.sum(raised, axis=0, keepdims=True)
            p = raised * (1.0 / total)
            pb = p.astype(BF)
            att[rows, sl] = left_dot(pb, vb).astype(BF)
            gp = right_dot(vb, gb)
            mid = jnp.sum(p * gp, axis=0, keepdims=True)
            ds = (p * (gp - mid) * SCALE).astype(BF)
            dq[rows, sl] = left_dot(ds, kb).astype(BF)
            own = slice(BLOCK, 3 * BLOCK) if b == 0 else slice(0, 2 * BLOCK)
            if tick == 0:
                dk_now, dv_now = dot(ds[own], qb), dot(pb[own], gb)
            else:
                far = slice(0, BLOCK) if b == 0 else slice(2 * BLOCK, 3 * BLOCK)
                dk_all, dv_all = dot(ds, qb), dot(pb, gb)
                pairs[2][rows, sl] = dk_all[far].astype(BF)
                pairs[3][rows, sl] = dv_all[far].astype(BF)
                dk_now, dv_now = dk_all[own], dv_all[own]
            dk_sum, dv_sum = (
                (dk_now, dv_now) if dk_sum is None else (dk_sum + dk_now, dv_sum + dv_now)
            )
            stats = (stats_first, stats_last)[b]
            stats[head : head + 1, :] = jnp.where(listed[b], peak, UNLISTED)
            stats[HEADS + head : HEADS + head + 1, :] = total
            stats[2 * HEADS + head : 2 * HEADS + head + 1, :] = mid
        dk[:, sl] = dk_sum
        dv[:, sl] = dv_sum
        if tick:
            pairs[0][:, sl] = dk_sum.astype(BF)
            pairs[1][:, sl] = dv_sum.astype(BF)


def attend(info, tick, q, k, v, kh, vh, wo, upstream):
    outs = [shape(ROWS, WIDE)] * 2 + [shape(ROWS, WIDE, F32)] * 2
    outs += [shape(3 * HEADS, BLOCK, F32)] * 2 + [shape(ROWS, WIDE)] * (5 * tick)
    return call(
        functools.partial(attend_kernel, tick),
        (info, q, k, v, kh, vh, wo, *upstream),
        outs,
        [],
        cost(8 * 2 * ROWS * WIDE * WIDE, 12 * ROWS * WIDE * 2),
        f"attend{tick}",
    )


def ahead_kernel(g_prev, g_next, wo, dq, wq, gah, part):
    g_far = jnp.concatenate([g_prev[:BLOCK, :], g_next[:BLOCK, :]], axis=0)
    gah[...] = right_dot(g_far, wo[...]).astype(BF)
    part[...] = right_dot(dq[...], wq[...])


def ahead(g_edges, wo, dq, wq, name):
    return call(
        ahead_kernel,
        (*g_edges, wo, dq, wq),
        [shape(ROWS, WIDE), shape(ROWS, WIDE, F32)],
        [],
        cost(4 * ROWS * WIDE * WIDE, 4 * WIDE * WIDE + 8 * ROWS * WIDE),
        name,
    )


def cross_kernel(tick, info, qh, gah, k, v, s_prev, s_next, dk, dv, gk, gv):
    base = tick * ROWS
    place = lax.broadcasted_iota(jnp.int32, (BLOCK, 1), 0)
    for head in range(HEADS):
        sl = slice(head * HEAD_DIM, (head + 1) * HEAD_DIM)
        for b, stats in enumerate((s_prev, s_next)):
            rows = slice(b * BLOCK, (b + 1) * BLOCK)
            mine = slice(base + b * BLOCK, base + (b + 1) * BLOCK)
            peak, total, mid = (
                stats[at * HEADS + head : at * HEADS + head + 1, :] for at in range(3)
            )
            qb, kb, vb, gb = qh[rows, sl], k[mine, sl], v[mine, sl], gah[rows, sl]
            s = right_dot(kb, qb) * SCALE
            inside = place < info[3 + 3 * b]
            p = jnp.where(inside, jnp.exp(s - peak), 0.0) * (1.0 / total)
            ds = (p * (right_dot(vb, gb) - mid) * SCALE).astype(BF)
            dk_far = dot(ds, qb).astype(BF).astype(F32)
            dv_far = dot(p.astype(BF), gb).astype(BF).astype(F32)
            gk[rows, sl] = (dk[rows, sl] + dk_far).astype(BF)
            gv[rows, sl] = (dv[rows, sl] + dv_far).astype(BF)


def cross(info, tick, qh, gah, k, v, stats, dk, dv):
    return call(
        functools.partial(cross_kernel, tick),
        (info, qh, gah, k, v, *stats, dk, dv),
        [shape(ROWS, WIDE)] * 2,
        [],
        cost(2 * ROWS * WIDE * WIDE, 20 * ROWS * WIDE),
        f"cross{tick}",
    )


def grad_kernel(tick, info, part, gk, gv, wk, wv, x, g, *rest):
    grad = part[...] + right_dot(gk[...], wk[...]) + right_dot(gv[...], wv[...])
    xf = x[...].astype(F32)
    r = inverse_rms(xf)
    xr = xf * r
    grad_in = r * (grad - xr * jnp.mean(grad * xr, axis=-1, keepdims=True))
    out = (g[...].astype(F32) + grad_in).astype(BF)
    if tick:
        earlier, gx = rest
        gx[0] = earlier[...]
        gx[1] = out
    else:
        top, gx, edge_last, edge_first = rest
        gx[...] = out
        at_bottom = info[1] == 0
        edge_last[...] = jnp.where(at_bottom, top[BLOCK:, :], out[BLOCK:, :])
        edge_first[...] = jnp.where(at_bottom, top[:BLOCK, :], out[:BLOCK, :])


def grad(info, tick, part, gk, gv, weights, x, gs):
    both = [jax.ShapeDtypeStruct((2, ROWS, WIDE), BF)]
    return call(
        functools.partial(grad_kernel, tick),
        (info, part, gk, gv, *weights[1:], x, *gs),
        both if tick else [shape(ROWS, WIDE)] + [shape(BLOCK, WIDE)] * 2,
        [],
        cost(4 * ROWS * WIDE * WIDE, 4 * WIDE * WIDE + 12 * ROWS * WIDE),
        f"grad{tick}",
    )


def position(order, q):
    found = 0
    for bit, mask in enumerate(order):
        if (q >> (len(order) - 1 - bit)) & 1:
            found ^= mask
    return found


def weight_kernel(order, offsets, info, *refs):
    count = len(offsets)
    lefts, rights, (keep, send, chunks) = refs[:count], refs[count : 2 * count], refs[2 * count :]
    product = sum(
        left_dot(left[offset : offset + ROWS, :], right[...])
        for left, offset, right in zip(lefts, offsets, rights)
    )
    chunks[...] = product.astype(BF).reshape(chunks.shape)
    me = info[0]
    half = PARTS // 2
    for q in range(PARTS):
        out = keep if q < half else send
        out[q % half] = chunks[lax.bitwise_xor(jnp.int32(position(order, q)), me)]


def weight_part(info, order, lefts, offsets, rights, name):
    half = jax.ShapeDtypeStruct((PARTS // 2, DEPTH, WIDE), BF)
    return call(
        functools.partial(weight_kernel, order, offsets),
        (info, *lefts, *rights),
        [half] * 2,
        [pltpu.VMEM((PARTS, DEPTH, WIDE), BF)],
        cost(4 * ROWS * WIDE * WIDE, 8 * ROWS * WIDE + 2 * WIDE * WIDE),
        name,
    )


def swap(value, mask):
    return lax.ppermute(value, "mesh", [(p, p ^ mask) for p in range(PARTS)])


def add(left, right):
    return (left.astype(F32) + right.astype(F32)).astype(BF)


def ring(value, steps):
    return lax.ppermute(value, "mesh", [(p, (p + steps) % PARTS) for p in range(PARTS)])


def from_above(value, sections, steps, cyclic):
    pairs = [
        (s * PARTS + p, (s - 1) % sections * PARTS + (p + steps) % PARTS)
        for s in range(0 if cyclic else 1, sections)
        for p in range(PARTS)
    ]
    return lax.ppermute(value, ("section", "mesh"), pairs)


def split_sum(keep, received):
    half = keep.shape[0] // 2
    return add(keep[:half], received[:half]), add(keep[half:], received[half:])


def per_device(
    saved_inputs, w_query, w_key, w_value, w_out, pending, top_grads, key_blocks, counts, plan
):
    sections = lax.axis_size("section")
    ids = jnp.stack([lax.axis_index("section"), lax.axis_index("mesh")]).astype(jnp.int32)
    weights = (w_query[0], w_key[0], w_value[0])
    wo = w_out[0]
    g0, top = pending[0], top_grads[0]
    info, last0, first0, x0, x1 = prepare(ids, plan, counts, key_blocks, saved_inputs[0])
    x_edges0 = (ring(last0, 1), ring(first0, -1))
    normed, q, k, v, later_last, later_first = project_own((x0, x1), g0, weights)
    later = (ring(later_last, 1), ring(later_first, -1))
    qh, kh, vh = project_edge(x_edges0, weights, False, "project_edge0")
    att0, dq0, dk, dv, stats_first, stats_last = attend(info, 0, q, k, v, kh, vh, wo, (g0,))
    stats = (ring(stats_last, 1), ring(stats_first, -1))
    gah, part = ahead(later, wo, dq0, weights[0], "ahead0")
    gk0, gv0 = cross(info, 0, qh, gah, k, v, stats, dk, dv)
    gx0, edge_last, edge_first = grad(info, 0, part, gk0, gv0, weights, x0, (g0, top))
    passed = from_above(gx0, sections, 0, False)
    qh, kh, vh, normed_far = project_edge(later, weights, True, "project_edge1")
    att1, dq1, dk, dv, stats_first, stats_last, g1, dk_own, dv_own, dk_far, dv_far = attend(
        info, 1, q, k, v, kh, vh, wo, (passed, top)
    )
    lefts = (normed, normed, normed_far)
    sums = []
    for w, left, offsets, right in (
        (1, lefts, (0, ROWS, 0), (gk0, dk_own, dk_far)),
        (2, lefts, (0, ROWS, 0), (gv0, dv_own, dv_far)),
        (0, (normed, normed), (0, ROWS), (dq0, dq1)),
        (3, (att0, att1), (0, 0), (g0, g1)),
    ):
        keep, send = weight_part(info, ORDERS[w], left, offsets, right, f"weight{w}")
        sums.append((w, keep, swap(send, ORDERS[w][0])))
    kept, (edge_last, edge_first) = lax.optimization_barrier(
        ([keep for _, keep, _ in sums], (edge_last, edge_first))
    )
    sums = [(w, keep, received) for (w, _, received), keep in zip(sums, kept)]
    g_edges1 = (
        from_above(edge_last, sections, 1, True),
        from_above(edge_first, sections, -1, True),
    )
    (g_edges1, stats_first, stats_last), received = lax.optimization_barrier(
        ((g_edges1, stats_first, stats_last), [received for _, _, received in sums])
    )
    sums = [(w, keep, got) for (w, keep, _), got in zip(sums, received)]
    stats = (ring(stats_last, 1), ring(stats_first, -1))
    gah, part = ahead(g_edges1, wo, dq1, weights[0], "ahead1")
    gk1, gv1 = cross(info, 1, qh, gah, k, v, stats, dk, dv)
    (gx,) = grad(info, 1, part, gk1, gv1, weights, x1, (g1, gx0))
    for stage in (1, 2, 3):
        pairs = [(w, *split_sum(keep, received)) for w, keep, received in sums]
        if stage == GRAD_BEFORE:
            gx, sends = lax.optimization_barrier((gx, [send for _, _, send in pairs]))
            pairs = [(w, keep, send) for (w, keep, _), send in zip(pairs, sends)]
        sums = [(w, keep, swap(send, ORDERS[w][stage])) for w, keep, send in pairs]
    totals = {}
    for group in (sums[:2], sums[2:]):
        pairs = [(w, *split_sum(keep, received)) for w, keep, received in group]
        far = swap(jnp.concatenate([send for _, _, send in pairs]), ZZ)
        for n, (w, keep, _) in enumerate(pairs):
            totals[w] = keep[0].astype(F32) + far[n].astype(F32)
    layer_total = jnp.stack([totals[w] for w in range(4)], axis=1)
    return (layer_total[None], gx[:, None])


def solution(mesh):
    in_specs = (
        P("section", None, "mesh", None),
        P("section", None, None),
        P("section", None, None),
        P("section", None, None),
        P("section", None, None),
        P("section", "mesh", None),
        P(None, "mesh", None),
        P("mesh", None),
        P(),
        P(),
    )
    out_specs = (P("section", "mesh", None, None), P(None, "section", "mesh", None))
    return jax.shard_map(
        per_device, mesh=mesh, in_specs=in_specs, out_specs=out_specs, check_vma=False
    )
```

```python
import functools
import math

import jax
import jax.numpy as jnp
from jax import lax
from jax.experimental import pallas as pl
from jax.experimental.pallas import tpu as pltpu
from jax.sharding import PartitionSpec as P

HEADS = 8
BLOCK = 128
ROWS = 256
WIDE = 1024
HEAD_DIM = 128
SECTIONS = 8
VMEM_LIMIT = 16 * 1024 * 1024
EPSILON = 1e-06
SCALE = 1.0 / math.sqrt(HEAD_DIM)
PARTS = 32
UNLISTED = 3e38
EDGES_BEFORE = (3,)
GRAD_BEFORE = 3
BF = jnp.bfloat16
F32 = jnp.float32

AX, BX, AY, BY, ZZ = 8, 24, 1, 3, 4
ORDERS = (
    (AX, AY, BX, BY, ZZ),
    (BX, BY, AX, AY, ZZ),
    (AY, AX, BY, BX, ZZ),
    (BY, BX, AY, AX, ZZ),
)
DEPTH = WIDE // PARTS


def right_dot(left, right):
    return lax.dot_general(
        left, right, (((1,), (1,)), ((), ())), preferred_element_type=jnp.float32
    )


def left_dot(left, right):
    return lax.dot_general(
        left, right, (((0,), (0,)), ((), ())), preferred_element_type=jnp.float32
    )


def dot(left, right):
    return jnp.dot(left, right, preferred_element_type=jnp.float32)


def inverse_rms(x):
    return lax.rsqrt(jnp.mean(x * x, axis=-1, keepdims=True) + EPSILON)


def cost(flops, moved):
    return pl.CostEstimate(flops=int(flops), bytes_accessed=int(moved), transcendentals=0)


def shape(rows, columns, dtype=BF):
    return jax.ShapeDtypeStruct((rows, columns), dtype)


def space(value):
    return pltpu.SMEM if value.dtype == jnp.int32 else pltpu.VMEM


def call(kernel, args, out_shape, scratch, estimate, name):
    return pl.pallas_call(
        kernel,
        out_shape=out_shape,
        in_specs=[pl.BlockSpec(memory_space=space(value)) for value in args],
        out_specs=[pl.BlockSpec(memory_space=space(value)) for value in out_shape],
        scratch_shapes=scratch,
        compiler_params=pltpu.CompilerParams(vmem_limit_bytes=VMEM_LIMIT),
        cost_estimate=estimate,
        name=name,
    )(*args)


def prepare_kernel(block_count, ints, saved, info, edge_last, edge_first, x0, x1):
    section, part = ints[0], ints[1]
    plan_at, counts_at, sections = 2, 2 + 2 * SECTIONS, SECTIONS
    blocks_at = counts_at + block_count
    first, last = slice(0, BLOCK), slice(ROWS - BLOCK, ROWS)
    m0, m1 = ints[plan_at + section], ints[plan_at + sections + section]
    edge_last[...] = saved[m0, last]
    edge_first[...] = saved[m0, first]
    x0[...] = saved[m0]
    x1[...] = saved[m1]
    info[0] = part
    info[1] = section
    for b in range(2):
        for e, j in ((0, 1), (2, 0)):
            listed = ints[blocks_at + 2 * b + j]
            found = ints[counts_at + jnp.maximum(listed, 0)]
            info[2 + 3 * b + e] = jnp.where(listed >= 0, found, 0)
        info[3 + 3 * b] = ints[counts_at + part * 2 + b]


def prepare(ids, plan, counts, key_blocks, saved):
    ints = jnp.concatenate([ids, plan.reshape(-1), counts, key_blocks.reshape(-1)])
    return call(
        functools.partial(prepare_kernel, counts.shape[0]),
        (ints, saved),
        [jax.ShapeDtypeStruct((8,), jnp.int32)]
        + [shape(BLOCK, WIDE)] * 2
        + [shape(ROWS, WIDE)] * 2,
        [],
        cost(0, 6 * ROWS * WIDE * 2),
        "prepare",
    )


def normalised(x):
    x = x.astype(F32)
    return (x * inverse_rms(x)).astype(BF)


def project_own_kernel(xa, xb, g, wq, wk, wv, normed_out, q, k, v, later_last, later_first):
    normed = jnp.concatenate([normalised(xa[...]), normalised(xb[...])], axis=0)
    normed_out[...] = normed
    for rows, later in ((slice(ROWS - BLOCK, ROWS), later_last), (slice(0, BLOCK), later_first)):
        later[:BLOCK, :] = g[rows, :]
        later[BLOCK:, :] = xb[rows, :]
    for weight, out in ((wq, q), (wk, k), (wv, v)):
        out[...] = dot(normed, weight[...]).astype(BF)


def project_own(xs, g, weights):
    rows = 2 * ROWS
    return call(
        project_own_kernel,
        (*xs, g, *weights),
        [shape(rows, WIDE)] * 4 + [shape(ROWS, WIDE)] * 2,
        [],
        cost(6 * rows * WIDE * WIDE, 6 * WIDE * WIDE + 10 * rows * WIDE),
        "project_own",
    )


def project_edge_kernel(xa, xb, wq, wk, wv, q, k, v, *normed_out):
    parts = [normalised(ref[ref.shape[0] - BLOCK :, :]) for ref in (xa, xb)]
    normed = jnp.concatenate(parts, axis=0)
    for out in normed_out:
        out[...] = normed
    for weight, out in ((wq, q), (wk, k), (wv, v)):
        out[...] = dot(normed, weight[...]).astype(BF)


def project_edge(xs, weights, keep_normed, name):
    return call(
        project_edge_kernel,
        (*xs, *weights),
        [shape(ROWS, WIDE)] * (3 + keep_normed),
        [],
        cost(6 * ROWS * WIDE * WIDE, 6 * WIDE * WIDE + 10 * ROWS * WIDE),
        name,
    )


def attend_kernel(tick, info, q, k, v, kh, vh, wo, *rest):
    if tick == 0:
        g, att, dq, dk, dv, stats_first, stats_last = rest
        upstream = g[...]
    else:
        g, top, att, dq, dk, dv, stats_first, stats_last, upstream_out, *pairs = rest
        upstream = jnp.where(info[1] == SECTIONS - 1, top[...], g[...])
        upstream_out[...] = upstream
    ga = right_dot(upstream, wo[...]).astype(BF)
    place = lax.broadcasted_iota(jnp.int32, (3 * BLOCK, 1), 0)
    base = tick * ROWS
    valid = []
    listed = []
    for b in range(2):
        limit = [info[2 + 3 * b + e] for e in range(3)]
        inside = place < jnp.minimum(limit[0], BLOCK)
        for e in (1, 2):
            at = place - e * BLOCK
            inside = inside | ((at >= 0) & (at < jnp.minimum(limit[e], BLOCK)))
        valid.append(inside)
        listed.append(limit[2 * b] > 0)
    for head in range(HEADS):
        sl = slice(head * HEAD_DIM, (head + 1) * HEAD_DIM)
        kx = jnp.concatenate([kh[:BLOCK, sl], k[base : base + ROWS, sl], kh[BLOCK:, sl]], axis=0)
        vx = jnp.concatenate([vh[:BLOCK, sl], v[base : base + ROWS, sl], vh[BLOCK:, sl]], axis=0)
        dk_sum = None
        for b in range(2):
            rows = slice(b * BLOCK, (b + 1) * BLOCK)
            qb, gb = q[base + b * BLOCK : base + (b + 1) * BLOCK, sl], ga[rows, sl]
            kb, vb = kx[b * BLOCK : (b + 3) * BLOCK], vx[b * BLOCK : (b + 3) * BLOCK]
            s = jnp.where(valid[b], right_dot(kb, qb) * SCALE, -jnp.inf)
            peak = jnp.max(s, axis=0, keepdims=True)
            raised = jnp.exp(s - peak)
            total = jnp.sum(raised, axis=0, keepdims=True)
            p = raised * (1.0 / total)
            pb = p.astype(BF)
            att[rows, sl] = left_dot(pb, vb).astype(BF)
            gp = right_dot(vb, gb)
            mid = jnp.sum(p * gp, axis=0, keepdims=True)
            ds = (p * (gp - mid) * SCALE).astype(BF)
            dq[rows, sl] = left_dot(ds, kb).astype(BF)
            own = slice(BLOCK, 3 * BLOCK) if b == 0 else slice(0, 2 * BLOCK)
            if tick == 0:
                dk_now, dv_now = dot(ds[own], qb), dot(pb[own], gb)
            else:
                far = slice(0, BLOCK) if b == 0 else slice(2 * BLOCK, 3 * BLOCK)
                dk_all, dv_all = dot(ds, qb), dot(pb, gb)
                pairs[2][rows, sl] = dk_all[far].astype(BF)
                pairs[3][rows, sl] = dv_all[far].astype(BF)
                dk_now, dv_now = dk_all[own], dv_all[own]
            dk_sum, dv_sum = (
                (dk_now, dv_now) if dk_sum is None else (dk_sum + dk_now, dv_sum + dv_now)
            )
            stats = (stats_first, stats_last)[b]
            stats[head : head + 1, :] = jnp.where(listed[b], peak, UNLISTED)
            stats[HEADS + head : HEADS + head + 1, :] = total
            stats[2 * HEADS + head : 2 * HEADS + head + 1, :] = mid
        dk[:, sl] = dk_sum
        dv[:, sl] = dv_sum
        if tick:
            pairs[0][:, sl] = dk_sum.astype(BF)
            pairs[1][:, sl] = dv_sum.astype(BF)


def attend(info, tick, q, k, v, kh, vh, wo, upstream):
    outs = [shape(ROWS, WIDE)] * 2 + [shape(ROWS, WIDE, F32)] * 2
    outs += [shape(3 * HEADS, BLOCK, F32)] * 2 + [shape(ROWS, WIDE)] * (5 * tick)
    return call(
        functools.partial(attend_kernel, tick),
        (info, q, k, v, kh, vh, wo, *upstream),
        outs,
        [],
        cost(8 * 2 * ROWS * WIDE * WIDE, 12 * ROWS * WIDE * 2),
        f"attend{tick}",
    )


def ahead_kernel(g_prev, g_next, wo, dq, wq, gah, part):
    g_far = jnp.concatenate([g_prev[:BLOCK, :], g_next[:BLOCK, :]], axis=0)
    gah[...] = right_dot(g_far, wo[...]).astype(BF)
    part[...] = right_dot(dq[...], wq[...])


def ahead(g_edges, wo, dq, wq, name):
    return call(
        ahead_kernel,
        (*g_edges, wo, dq, wq),
        [shape(ROWS, WIDE), shape(ROWS, WIDE, F32)],
        [],
        cost(4 * ROWS * WIDE * WIDE, 4 * WIDE * WIDE + 8 * ROWS * WIDE),
        name,
    )


def cross_kernel(tick, info, qh, gah, k, v, s_prev, s_next, dk, dv, gk, gv):
    base = tick * ROWS
    place = lax.broadcasted_iota(jnp.int32, (BLOCK, 1), 0)
    for head in range(HEADS):
        sl = slice(head * HEAD_DIM, (head + 1) * HEAD_DIM)
        for b, stats in enumerate((s_prev, s_next)):
            rows = slice(b * BLOCK, (b + 1) * BLOCK)
            mine = slice(base + b * BLOCK, base + (b + 1) * BLOCK)
            peak, total, mid = (
                stats[at * HEADS + head : at * HEADS + head + 1, :] for at in range(3)
            )
            qb, kb, vb, gb = qh[rows, sl], k[mine, sl], v[mine, sl], gah[rows, sl]
            s = right_dot(kb, qb) * SCALE
            inside = place < info[3 + 3 * b]
            p = jnp.where(inside, jnp.exp(s - peak), 0.0) * (1.0 / total)
            ds = (p * (right_dot(vb, gb) - mid) * SCALE).astype(BF)
            dk_far = dot(ds, qb).astype(BF).astype(F32)
            dv_far = dot(p.astype(BF), gb).astype(BF).astype(F32)
            gk[rows, sl] = (dk[rows, sl] + dk_far).astype(BF)
            gv[rows, sl] = (dv[rows, sl] + dv_far).astype(BF)


def cross(info, tick, qh, gah, k, v, stats, dk, dv):
    return call(
        functools.partial(cross_kernel, tick),
        (info, qh, gah, k, v, *stats, dk, dv),
        [shape(ROWS, WIDE)] * 2,
        [],
        cost(2 * ROWS * WIDE * WIDE, 20 * ROWS * WIDE),
        f"cross{tick}",
    )


def grad_kernel(tick, info, part, gk, gv, wk, wv, x, g, *rest):
    grad = part[...] + right_dot(gk[...], wk[...]) + right_dot(gv[...], wv[...])
    xf = x[...].astype(F32)
    r = inverse_rms(xf)
    xr = xf * r
    grad_in = r * (grad - xr * jnp.mean(grad * xr, axis=-1, keepdims=True))
    out = (g[...].astype(F32) + grad_in).astype(BF)
    if tick:
        earlier, gx = rest
        gx[0] = earlier[...]
        gx[1] = out
    else:
        top, gx, edge_last, edge_first = rest
        gx[...] = out
        at_bottom = info[1] == 0
        edge_last[...] = jnp.where(at_bottom, top[BLOCK:, :], out[BLOCK:, :])
        edge_first[...] = jnp.where(at_bottom, top[:BLOCK, :], out[:BLOCK, :])


def grad(info, tick, part, gk, gv, weights, x, gs):
    both = [jax.ShapeDtypeStruct((2, ROWS, WIDE), BF)]
    return call(
        functools.partial(grad_kernel, tick),
        (info, part, gk, gv, *weights[1:], x, *gs),
        both if tick else [shape(ROWS, WIDE)] + [shape(BLOCK, WIDE)] * 2,
        [],
        cost(4 * ROWS * WIDE * WIDE, 4 * WIDE * WIDE + 12 * ROWS * WIDE),
        f"grad{tick}",
    )


def position(order, q):
    found = 0
    for bit, mask in enumerate(order):
        if (q >> (len(order) - 1 - bit)) & 1:
            found ^= mask
    return found


def weight_kernel(order, offsets, info, *refs):
    count = len(offsets)
    lefts, rights, (keep, send, chunks) = refs[:count], refs[count : 2 * count], refs[2 * count :]
    product = sum(
        left_dot(left[offset : offset + ROWS, :], right[...])
        for left, offset, right in zip(lefts, offsets, rights)
    )
    chunks[...] = product.astype(BF).reshape(chunks.shape)
    me = info[0]
    half = PARTS // 2
    for q in range(PARTS):
        out = keep if q < half else send
        out[q % half] = chunks[lax.bitwise_xor(jnp.int32(position(order, q)), me)]


def weight_part(info, order, lefts, offsets, rights, name):
    half = jax.ShapeDtypeStruct((PARTS // 2, DEPTH, WIDE), BF)
    return call(
        functools.partial(weight_kernel, order, offsets),
        (info, *lefts, *rights),
        [half] * 2,
        [pltpu.VMEM((PARTS, DEPTH, WIDE), BF)],
        cost(4 * ROWS * WIDE * WIDE, 8 * ROWS * WIDE + 2 * WIDE * WIDE),
        name,
    )


def swap(value, mask):
    return lax.ppermute(value, "mesh", [(p, p ^ mask) for p in range(PARTS)])


def add(left, right):
    return (left.astype(F32) + right.astype(F32)).astype(BF)


def ring(value, steps):
    return lax.ppermute(value, "mesh", [(p, (p + steps) % PARTS) for p in range(PARTS)])


def from_above(value, sections, steps, cyclic):
    pairs = [
        (s * PARTS + p, (s - 1) % sections * PARTS + (p + steps) % PARTS)
        for s in range(0 if cyclic else 1, sections)
        for p in range(PARTS)
    ]
    return lax.ppermute(value, ("section", "mesh"), pairs)


def split_sum(keep, received):
    half = keep.shape[0] // 2
    return add(keep[:half], received[:half]), add(keep[half:], received[half:])


def per_device(
    saved_inputs, w_query, w_key, w_value, w_out, pending, top_grads, key_blocks, counts, plan
):
    sections = lax.axis_size("section")
    ids = jnp.stack([lax.axis_index("section"), lax.axis_index("mesh")]).astype(jnp.int32)
    weights = (w_query[0], w_key[0], w_value[0])
    wo = w_out[0]
    g0, top = pending[0], top_grads[0]
    info, last0, first0, x0, x1 = prepare(ids, plan, counts, key_blocks, saved_inputs[0])
    x_edges0 = (ring(last0, 1), ring(first0, -1))
    normed, q, k, v, later_last, later_first = project_own((x0, x1), g0, weights)
    later = (ring(later_last, 1), ring(later_first, -1))
    qh, kh, vh = project_edge(x_edges0, weights, False, "project_edge0")
    att0, dq0, dk, dv, stats_first, stats_last = attend(info, 0, q, k, v, kh, vh, wo, (g0,))
    stats = (ring(stats_last, 1), ring(stats_first, -1))
    gah, part = ahead(later, wo, dq0, weights[0], "ahead0")
    gk0, gv0 = cross(info, 0, qh, gah, k, v, stats, dk, dv)
    gx0, edge_last, edge_first = grad(info, 0, part, gk0, gv0, weights, x0, (g0, top))
    passed = from_above(gx0, sections, 0, False)
    qh, kh, vh, normed_far = project_edge(later, weights, True, "project_edge1")
    g_edges1 = (
        from_above(edge_last, sections, 1, True),
        from_above(edge_first, sections, -1, True),
    )
    att1, dq1, dk, dv, stats_first, stats_last, g1, dk_own, dv_own, dk_far, dv_far = attend(
        info, 1, q, k, v, kh, vh, wo, (passed, top)
    )
    lefts = (normed, normed, normed_far)
    sums = []
    for w, left, offsets, right in (
        (1, lefts, (0, ROWS, 0), (gk0, dk_own, dk_far)),
        (2, lefts, (0, ROWS, 0), (gv0, dv_own, dv_far)),
        (0, (normed, normed), (0, ROWS), (dq0, dq1)),
        (3, (att0, att1), (0, 0), (g0, g1)),
    ):
        if w in EDGES_BEFORE:
            g_edges1, right = lax.optimization_barrier((g_edges1, right))
        keep, send = weight_part(info, ORDERS[w], left, offsets, right, f"weight{w}")
        sums.append((w, keep, swap(send, ORDERS[w][0])))
    (stats_first, stats_last), received = lax.optimization_barrier(
        ((stats_first, stats_last), [received for _, _, received in sums])
    )
    sums = [(w, keep, got) for (w, keep, _), got in zip(sums, received)]
    stats = (ring(stats_last, 1), ring(stats_first, -1))
    gah, part = ahead(g_edges1, wo, dq1, weights[0], "ahead1")
    gk1, gv1 = cross(info, 1, qh, gah, k, v, stats, dk, dv)
    (gx,) = grad(info, 1, part, gk1, gv1, weights, x1, (g1, gx0))
    for stage in (1, 2, 3):
        pairs = [(w, *split_sum(keep, received)) for w, keep, received in sums]
        if stage == GRAD_BEFORE:
            gx, sends = lax.optimization_barrier((gx, [send for _, _, send in pairs]))
            pairs = [(w, keep, send) for (w, keep, _), send in zip(pairs, sends)]
        sums = [(w, keep, swap(send, ORDERS[w][stage])) for w, keep, send in pairs]
    totals = {}
    for group in (sums[:2], sums[2:]):
        pairs = [(w, *split_sum(keep, received)) for w, keep, received in group]
        far = swap(jnp.concatenate([send for _, _, send in pairs]), ZZ)
        for n, (w, keep, _) in enumerate(pairs):
            totals[w] = keep[0].astype(F32) + far[n].astype(F32)
    layer_total = jnp.stack([totals[w] for w in range(4)], axis=1)
    return (layer_total[None], gx[:, None])


def solution(mesh):
    in_specs = (
        P("section", None, "mesh", None),
        P("section", None, None),
        P("section", None, None),
        P("section", None, None),
        P("section", None, None),
        P("section", "mesh", None),
        P(None, "mesh", None),
        P("mesh", None),
        P(),
        P(),
    )
    out_specs = (P("section", "mesh", None, None), P(None, "section", "mesh", None))
    return jax.shard_map(
        per_device, mesh=mesh, in_specs=in_specs, out_specs=out_specs, check_vma=False
    )
```

```python
import functools
import math

import jax
import jax.numpy as jnp
from jax import lax
from jax.experimental import pallas as pl
from jax.experimental.pallas import tpu as pltpu
from jax.sharding import PartitionSpec as P

HEADS = 8
BLOCK = 128
ROWS = 256
WIDE = 1024
HEAD_DIM = 128
SECTIONS = 8
VMEM_LIMIT = 16 * 1024 * 1024
EPSILON = 1e-06
SCALE = 1.0 / math.sqrt(HEAD_DIM)
PARTS = 32
UNLISTED = 3e38
EDGES_BEFORE = (3,)
GRAD_BEFORE = 3
BF = jnp.bfloat16
F32 = jnp.float32

AX, BX, AY, BY, ZZ = 8, 24, 1, 3, 4
ORDERS = (
    (AX, AY, BX, BY, ZZ),
    (BX, BY, AX, AY, ZZ),
    (AY, AX, BY, BX, ZZ),
    (BY, BX, AY, AX, ZZ),
)
DEPTH = WIDE // PARTS


def right_dot(left, right):
    return lax.dot_general(
        left, right, (((1,), (1,)), ((), ())), preferred_element_type=jnp.float32
    )


def left_dot(left, right):
    return lax.dot_general(
        left, right, (((0,), (0,)), ((), ())), preferred_element_type=jnp.float32
    )


def dot(left, right):
    return jnp.dot(left, right, preferred_element_type=jnp.float32)


def inverse_rms(x):
    return lax.rsqrt(jnp.mean(x * x, axis=-1, keepdims=True) + EPSILON)


def cost(flops, moved):
    return pl.CostEstimate(flops=int(flops), bytes_accessed=int(moved), transcendentals=0)


def shape(rows, columns, dtype=BF):
    return jax.ShapeDtypeStruct((rows, columns), dtype)


def space(value):
    return pltpu.SMEM if value.dtype == jnp.int32 else pltpu.VMEM


def call(kernel, args, out_shape, scratch, estimate, name):
    return pl.pallas_call(
        kernel,
        out_shape=out_shape,
        in_specs=[pl.BlockSpec(memory_space=space(value)) for value in args],
        out_specs=[pl.BlockSpec(memory_space=space(value)) for value in out_shape],
        scratch_shapes=scratch,
        compiler_params=pltpu.CompilerParams(vmem_limit_bytes=VMEM_LIMIT),
        cost_estimate=estimate,
        name=name,
    )(*args)


def prepare_kernel(block_count, ints, saved, info, edge_last, edge_first, x0, x1):
    section, part = ints[0], ints[1]
    plan_at, counts_at, sections = 2, 2 + 2 * SECTIONS, SECTIONS
    blocks_at = counts_at + block_count
    first, last = slice(0, BLOCK), slice(ROWS - BLOCK, ROWS)
    m0, m1 = ints[plan_at + section], ints[plan_at + sections + section]
    edge_last[...] = saved[m0, last]
    edge_first[...] = saved[m0, first]
    x0[...] = saved[m0]
    x1[...] = saved[m1]
    info[0] = part
    info[1] = section
    for b in range(2):
        for e, j in ((0, 1), (2, 0)):
            listed = ints[blocks_at + 2 * b + j]
            found = ints[counts_at + jnp.maximum(listed, 0)]
            info[2 + 3 * b + e] = jnp.where(listed >= 0, found, 0)
        info[3 + 3 * b] = ints[counts_at + part * 2 + b]


def prepare(ids, plan, counts, key_blocks, saved):
    ints = jnp.concatenate([ids, plan.reshape(-1), counts, key_blocks.reshape(-1)])
    return call(
        functools.partial(prepare_kernel, counts.shape[0]),
        (ints, saved),
        [jax.ShapeDtypeStruct((8,), jnp.int32)]
        + [shape(BLOCK, WIDE)] * 2
        + [shape(ROWS, WIDE)] * 2,
        [],
        cost(0, 6 * ROWS * WIDE * 2),
        "prepare",
    )


def normalised(x):
    x = x.astype(F32)
    return (x * inverse_rms(x)).astype(BF)


def project_own_kernel(xa, xb, g, wq, wk, wv, normed_out, q, k, v, later_last, later_first):
    normed = jnp.concatenate([normalised(xa[...]), normalised(xb[...])], axis=0)
    normed_out[...] = normed
    for rows, later in ((slice(ROWS - BLOCK, ROWS), later_last), (slice(0, BLOCK), later_first)):
        later[:BLOCK, :] = g[rows, :]
        later[BLOCK:, :] = xb[rows, :]
    for weight, out in ((wq, q), (wk, k), (wv, v)):
        out[...] = dot(normed, weight[...]).astype(BF)


def project_own(xs, g, weights):
    rows = 2 * ROWS
    return call(
        project_own_kernel,
        (*xs, g, *weights),
        [shape(rows, WIDE)] * 4 + [shape(ROWS, WIDE)] * 2,
        [],
        cost(6 * rows * WIDE * WIDE, 6 * WIDE * WIDE + 10 * rows * WIDE),
        "project_own",
    )


def project_edge_kernel(xa, xb, wq, wk, wv, q, k, v, *normed_out):
    parts = [normalised(ref[ref.shape[0] - BLOCK :, :]) for ref in (xa, xb)]
    normed = jnp.concatenate(parts, axis=0)
    for out in normed_out:
        out[...] = normed
    for weight, out in ((wq, q), (wk, k), (wv, v)):
        out[...] = dot(normed, weight[...]).astype(BF)


def project_edge(xs, weights, keep_normed, name):
    return call(
        project_edge_kernel,
        (*xs, *weights),
        [shape(ROWS, WIDE)] * (3 + keep_normed),
        [],
        cost(6 * ROWS * WIDE * WIDE, 6 * WIDE * WIDE + 10 * ROWS * WIDE),
        name,
    )


def attend_kernel(tick, info, q, k, v, kh, vh, wo, *rest):
    if tick == 0:
        g, att, dq, dk, dv, stats_first, stats_last = rest
        upstream = g[...]
    else:
        g, top, att, dq, dk, dv, stats_first, stats_last, upstream_out, *pairs = rest
        upstream = jnp.where(info[1] == SECTIONS - 1, top[...], g[...])
        upstream_out[...] = upstream
    ga = right_dot(upstream, wo[...]).astype(BF)
    place = lax.broadcasted_iota(jnp.int32, (3 * BLOCK, 1), 0)
    base = tick * ROWS
    valid = []
    listed = []
    for b in range(2):
        limit = [info[2 + 3 * b + e] for e in range(3)]
        inside = place < jnp.minimum(limit[0], BLOCK)
        for e in (1, 2):
            at = place - e * BLOCK
            inside = inside | ((at >= 0) & (at < jnp.minimum(limit[e], BLOCK)))
        valid.append(inside)
        listed.append(limit[2 * b] > 0)
    for head in range(HEADS):
        sl = slice(head * HEAD_DIM, (head + 1) * HEAD_DIM)
        kx = jnp.concatenate([kh[:BLOCK, sl], k[base : base + ROWS, sl], kh[BLOCK:, sl]], axis=0)
        vx = jnp.concatenate([vh[:BLOCK, sl], v[base : base + ROWS, sl], vh[BLOCK:, sl]], axis=0)
        dk_sum = None
        for b in range(2):
            rows = slice(b * BLOCK, (b + 1) * BLOCK)
            qb, gb = q[base + b * BLOCK : base + (b + 1) * BLOCK, sl], ga[rows, sl]
            kb, vb = kx[b * BLOCK : (b + 3) * BLOCK], vx[b * BLOCK : (b + 3) * BLOCK]
            s = jnp.where(valid[b], right_dot(kb, qb) * SCALE, -jnp.inf)
            peak = jnp.max(s, axis=0, keepdims=True)
            raised = jnp.exp(s - peak)
            total = jnp.sum(raised, axis=0, keepdims=True)
            p = raised * (1.0 / total)
            pb = p.astype(BF)
            att[rows, sl] = left_dot(pb, vb).astype(BF)
            gp = right_dot(vb, gb)
            mid = jnp.sum(p * gp, axis=0, keepdims=True)
            ds = (p * (gp - mid) * SCALE).astype(BF)
            dq[rows, sl] = left_dot(ds, kb).astype(BF)
            own = slice(BLOCK, 3 * BLOCK) if b == 0 else slice(0, 2 * BLOCK)
            if tick == 0:
                dk_now, dv_now = dot(ds[own], qb), dot(pb[own], gb)
            else:
                far = slice(0, BLOCK) if b == 0 else slice(2 * BLOCK, 3 * BLOCK)
                dk_all, dv_all = dot(ds, qb), dot(pb, gb)
                pairs[2][rows, sl] = dk_all[far].astype(BF)
                pairs[3][rows, sl] = dv_all[far].astype(BF)
                dk_now, dv_now = dk_all[own], dv_all[own]
            dk_sum, dv_sum = (
                (dk_now, dv_now) if dk_sum is None else (dk_sum + dk_now, dv_sum + dv_now)
            )
            stats = (stats_first, stats_last)[b]
            stats[head : head + 1, :] = jnp.where(listed[b], peak, UNLISTED)
            stats[HEADS + head : HEADS + head + 1, :] = total
            stats[2 * HEADS + head : 2 * HEADS + head + 1, :] = mid
        dk[:, sl] = dk_sum
        dv[:, sl] = dv_sum
        if tick:
            pairs[0][:, sl] = dk_sum.astype(BF)
            pairs[1][:, sl] = dv_sum.astype(BF)


def attend(info, tick, q, k, v, kh, vh, wo, upstream):
    outs = [shape(ROWS, WIDE)] * 2 + [shape(ROWS, WIDE, F32)] * 2
    outs += [shape(3 * HEADS, BLOCK, F32)] * 2 + [shape(ROWS, WIDE)] * (5 * tick)
    return call(
        functools.partial(attend_kernel, tick),
        (info, q, k, v, kh, vh, wo, *upstream),
        outs,
        [],
        cost(8 * 2 * ROWS * WIDE * WIDE, 12 * ROWS * WIDE * 2),
        f"attend{tick}",
    )


def ahead_kernel(g_prev, g_next, wo, dq, wq, gah, part):
    g_far = jnp.concatenate([g_prev[:BLOCK, :], g_next[:BLOCK, :]], axis=0)
    gah[...] = right_dot(g_far, wo[...]).astype(BF)
    part[...] = right_dot(dq[...], wq[...])


def ahead(g_edges, wo, dq, wq, name):
    return call(
        ahead_kernel,
        (*g_edges, wo, dq, wq),
        [shape(ROWS, WIDE), shape(ROWS, WIDE, F32)],
        [],
        cost(4 * ROWS * WIDE * WIDE, 4 * WIDE * WIDE + 8 * ROWS * WIDE),
        name,
    )


def cross_kernel(tick, info, qh, gah, k, v, s_prev, s_next, dk, dv, gk, gv):
    base = tick * ROWS
    place = lax.broadcasted_iota(jnp.int32, (BLOCK, 1), 0)
    for head in range(HEADS):
        sl = slice(head * HEAD_DIM, (head + 1) * HEAD_DIM)
        for b, stats in enumerate((s_prev, s_next)):
            rows = slice(b * BLOCK, (b + 1) * BLOCK)
            mine = slice(base + b * BLOCK, base + (b + 1) * BLOCK)
            peak, total, mid = (
                stats[at * HEADS + head : at * HEADS + head + 1, :] for at in range(3)
            )
            qb, kb, vb, gb = qh[rows, sl], k[mine, sl], v[mine, sl], gah[rows, sl]
            s = right_dot(kb, qb) * SCALE
            inside = place < info[3 + 3 * b]
            p = jnp.where(inside, jnp.exp(s - peak), 0.0) * (1.0 / total)
            ds = (p * (right_dot(vb, gb) - mid) * SCALE).astype(BF)
            dk_far = dot(ds, qb).astype(BF).astype(F32)
            dv_far = dot(p.astype(BF), gb).astype(BF).astype(F32)
            gk[rows, sl] = (dk[rows, sl] + dk_far).astype(BF)
            gv[rows, sl] = (dv[rows, sl] + dv_far).astype(BF)


def cross(info, tick, qh, gah, k, v, stats, dk, dv):
    return call(
        functools.partial(cross_kernel, tick),
        (info, qh, gah, k, v, *stats, dk, dv),
        [shape(ROWS, WIDE)] * 2,
        [],
        cost(2 * ROWS * WIDE * WIDE, 20 * ROWS * WIDE),
        f"cross{tick}",
    )


def grad_kernel(tick, info, part, gk, gv, wk, wv, x, g, *rest):
    grad = part[...] + right_dot(gk[...], wk[...]) + right_dot(gv[...], wv[...])
    xf = x[...].astype(F32)
    r = inverse_rms(xf)
    xr = xf * r
    grad_in = r * (grad - xr * jnp.mean(grad * xr, axis=-1, keepdims=True))
    out = (g[...].astype(F32) + grad_in).astype(BF)
    if tick:
        earlier, gx = rest
        gx[0] = earlier[...]
        gx[1] = out
    else:
        top, gx, edge_last, edge_first = rest
        gx[...] = out
        at_bottom = info[1] == 0
        edge_last[...] = jnp.where(at_bottom, top[BLOCK:, :], out[BLOCK:, :])
        edge_first[...] = jnp.where(at_bottom, top[:BLOCK, :], out[:BLOCK, :])


def grad(info, tick, part, gk, gv, weights, x, gs):
    both = [jax.ShapeDtypeStruct((2, ROWS, WIDE), BF)]
    return call(
        functools.partial(grad_kernel, tick),
        (info, part, gk, gv, *weights[1:], x, *gs),
        both if tick else [shape(ROWS, WIDE)] + [shape(BLOCK, WIDE)] * 2,
        [],
        cost(4 * ROWS * WIDE * WIDE, 4 * WIDE * WIDE + 12 * ROWS * WIDE),
        f"grad{tick}",
    )


def position(order, q):
    found = 0
    for bit, mask in enumerate(order):
        if (q >> (len(order) - 1 - bit)) & 1:
            found ^= mask
    return found


def weight_kernel(order, offsets, info, *refs):
    count = len(offsets)
    lefts, rights, (keep, send, chunks) = refs[:count], refs[count : 2 * count], refs[2 * count :]
    product = sum(
        left_dot(left[offset : offset + ROWS, :], right[...])
        for left, offset, right in zip(lefts, offsets, rights)
    )
    chunks[...] = product.astype(BF).reshape(chunks.shape)
    me = info[0]
    half = PARTS // 2
    for q in range(PARTS):
        out = keep if q < half else send
        out[q % half] = chunks[lax.bitwise_xor(jnp.int32(position(order, q)), me)]


def weight_part(info, order, lefts, offsets, rights, name):
    half = jax.ShapeDtypeStruct((PARTS // 2, DEPTH, WIDE), BF)
    return call(
        functools.partial(weight_kernel, order, offsets),
        (info, *lefts, *rights),
        [half] * 2,
        [pltpu.VMEM((PARTS, DEPTH, WIDE), BF)],
        cost(4 * ROWS * WIDE * WIDE, 8 * ROWS * WIDE + 2 * WIDE * WIDE),
        name,
    )


def swap(value, mask):
    return lax.ppermute(value, "mesh", [(p, p ^ mask) for p in range(PARTS)])


def add(left, right):
    return (left.astype(F32) + right.astype(F32)).astype(BF)


def ring(value, steps):
    return lax.ppermute(value, "mesh", [(p, (p + steps) % PARTS) for p in range(PARTS)])


def from_above(value, sections, steps, cyclic):
    pairs = [
        (s * PARTS + p, (s - 1) % sections * PARTS + (p + steps) % PARTS)
        for s in range(0 if cyclic else 1, sections)
        for p in range(PARTS)
    ]
    return lax.ppermute(value, ("section", "mesh"), pairs)


def split_sum(keep, received):
    half = keep.shape[0] // 2
    return add(keep[:half], received[:half]), add(keep[half:], received[half:])


def per_device(
    saved_inputs, w_query, w_key, w_value, w_out, pending, top_grads, key_blocks, counts, plan
):
    sections = lax.axis_size("section")
    ids = jnp.stack([lax.axis_index("section"), lax.axis_index("mesh")]).astype(jnp.int32)
    weights = (w_query[0], w_key[0], w_value[0])
    wo = w_out[0]
    g0, top = pending[0], top_grads[0]
    info, last0, first0, x0, x1 = prepare(ids, plan, counts, key_blocks, saved_inputs[0])
    x_edges0 = (ring(last0, 1), ring(first0, -1))
    normed, q, k, v, later_last, later_first = project_own((x0, x1), g0, weights)
    later = (ring(later_last, 1), ring(later_first, -1))
    qh, kh, vh = project_edge(x_edges0, weights, False, "project_edge0")
    att0, dq0, dk, dv, stats_first, stats_last = attend(info, 0, q, k, v, kh, vh, wo, (g0,))
    stats = (ring(stats_last, 1), ring(stats_first, -1))
    gah, part = ahead(later, wo, dq0, weights[0], "ahead0")
    gk0, gv0 = cross(info, 0, qh, gah, k, v, stats, dk, dv)
    gx0, edge_last, edge_first = grad(info, 0, part, gk0, gv0, weights, x0, (g0, top))
    passed = from_above(gx0, sections, 0, False)
    qh, kh, vh, normed_far = project_edge(later, weights, True, "project_edge1")
    g_edges1 = (
        from_above(edge_last, sections, 1, True),
        from_above(edge_first, sections, -1, True),
    )
    att1, dq1, dk, dv, stats_first, stats_last, g1, dk_own, dv_own, dk_far, dv_far = attend(
        info, 1, q, k, v, kh, vh, wo, (passed, top)
    )
    lefts = (normed, normed, normed_far)
    sums = []
    for w, left, offsets, right in (
        (1, lefts, (0, ROWS, 0), (gk0, dk_own, dk_far)),
        (2, lefts, (0, ROWS, 0), (gv0, dv_own, dv_far)),
        (0, (normed, normed), (0, ROWS), (dq0, dq1)),
        (3, (att0, att1), (0, 0), (g0, g1)),
    ):
        if w in EDGES_BEFORE:
            g_edges1, right = lax.optimization_barrier((g_edges1, right))
        keep, send = weight_part(info, ORDERS[w], left, offsets, right, f"weight{w}")
        sums.append((w, keep, swap(send, ORDERS[w][0])))
    (stats_first, stats_last), received = lax.optimization_barrier(
        ((stats_first, stats_last), [received for _, _, received in sums[:2]])
    )
    sums[:2] = [(w, keep, got) for (w, keep, _), got in zip(sums[:2], received)]
    stats = (ring(stats_last, 1), ring(stats_first, -1))
    gah, part = ahead(g_edges1, wo, dq1, weights[0], "ahead1")
    gk1, gv1 = cross(info, 1, qh, gah, k, v, stats, dk, dv)
    (gx,) = grad(info, 1, part, gk1, gv1, weights, x1, (g1, gx0))
    for stage in (1, 2, 3):
        pairs = [(w, *split_sum(keep, received)) for w, keep, received in sums]
        if stage == GRAD_BEFORE:
            gx, sends = lax.optimization_barrier((gx, [send for _, _, send in pairs]))
            pairs = [(w, keep, send) for (w, keep, _), send in zip(pairs, sends)]
        sums = [(w, keep, swap(send, ORDERS[w][stage])) for w, keep, send in pairs]
    totals = {}
    for group in (sums[:2], sums[2:]):
        pairs = [(w, *split_sum(keep, received)) for w, keep, received in group]
        far = swap(jnp.concatenate([send for _, _, send in pairs]), ZZ)
        for n, (w, keep, _) in enumerate(pairs):
            totals[w] = keep[0].astype(F32) + far[n].astype(F32)
    layer_total = jnp.stack([totals[w] for w in range(4)], axis=1)
    return (layer_total[None], gx[:, None])


def solution(mesh):
    in_specs = (
        P("section", None, "mesh", None),
        P("section", None, None),
        P("section", None, None),
        P("section", None, None),
        P("section", None, None),
        P("section", "mesh", None),
        P(None, "mesh", None),
        P("mesh", None),
        P(),
        P(),
    )
    out_specs = (P("section", "mesh", None, None), P(None, "section", "mesh", None))
    return jax.shard_map(
        per_device, mesh=mesh, in_specs=in_specs, out_specs=out_specs, check_vma=False
    )
```
